128 devices in a mesh: users: 32 (over x_hi, y, z), items: 4 (over x_lo, core).
Axes of the slice: x: 4 (x_hi: 2, x_lo: 2; x = x_hi * 2 + x_lo), y: 4, z: 4, core: 2. Of those that a mesh axis runs over, the one named last changes fastest.
Arguments:
- tile_rows: int32 [32, 4, 512], P('users', 'items'), may hold values from 0 to 63, as said below
- tile_cols: int32 [32, 4, 512], P('users', 'items'), may hold values from 0 to 63, as said below
- tile_count: int32 [32, 4], P('users', 'items'), may hold values from 64 to 512, as said below
- tile_vals: bfloat16 [32, 4, 512, 128, 128], P('users', 'items'), may hold values from -6 to 6
- user_degree: int32 [262144], P(('users', 'items')), may hold values from 16 to 575
- item_degree: int32 [32768], P(('items', 'users')), may hold values from 16 to 575
- start_items: bfloat16 [64, 32768], P(None, ('items', 'users')), may hold values from -6 to 6
Outputs:
- user_panel: float32 [64, 262144], P(None, ('users', 'items'))
- item_panel: float32 [64, 32768], P(None, ('items', 'users'))
The draws below stay inside these ranges and needn't reach their ends.
Inputs may be any that keep to these rules, and one draw needn't show every extreme that they name: Within one user block and item block, the pairs (tile_rows, tile_cols) of all 512 slots are distinct. `tile_cols`: paired with tile_rows slot by slot. Only the first tile_count slots of a block are live; some block is full in every draw.
All inputs are finite; a program needn't handle non-finite values.
Results may differ from the reference program's by a relative error of at most 0.0003.
Values sent between devices are 32-bit elements; how exact they have to be, the bound alone decides.
A program may use at most 128 MiB of HBM per device.

```python
import jax
import jax.numpy as jnp
from jax import lax

K = 64
TILE = 128
ITERS = 2
UT = 64
IT = 64
TILES_DEV = 512
USER_BLOCKS = 32
ITEM_BLOCKS = 4
USERS = 262144
ITEMS = 32768


def tile_slots(key):
    base = jax.random.fold_in(key, 7)
    keys = jax.random.split(base, USER_BLOCKS * ITEM_BLOCKS)
    chosen = jax.vmap(lambda single: jax.random.permutation(single, UT * IT)[:TILES_DEV])(keys)
    return chosen.reshape(USER_BLOCKS, ITEM_BLOCKS, TILES_DEV).astype(jnp.int32)


def draw_tile_rows(key, part):
    return tile_slots(key) // IT


def draw_tile_cols(key, part):
    return tile_slots(key) % IT


def draw_tile_count(key, part):
    first = jax.random.fold_in(key, 11)
    second = jax.random.fold_in(key, 13)
    powers = jax.random.randint(first, (USER_BLOCKS * ITEM_BLOCKS,), 0, 4)
    counts = jnp.maximum(TILES_DEV // jnp.left_shift(jnp.int32(1), powers.astype(jnp.int32)), 1)
    fullest = jax.random.randint(second, (), 0, USER_BLOCKS * ITEM_BLOCKS)
    counts = jnp.where(jnp.arange(USER_BLOCKS * ITEM_BLOCKS) == fullest, TILES_DEV, counts)
    return counts.reshape(USER_BLOCKS, ITEM_BLOCKS).astype(jnp.int32)


def degree_draw(key, total):
    base = jax.random.randint(key, (total,), 16, 64)
    places = jnp.arange(total, dtype=jnp.int32)
    return (base * (total + 8 * places) // total).astype(jnp.int32)


def draw_user_degree(key, part):
    return degree_draw(jax.random.fold_in(key, 17), USERS)


def draw_item_degree(key, part):
    return degree_draw(jax.random.fold_in(key, 19), ITEMS)


def steps_of(stream_key, shape, shards, low, high):
    factor_of = 1.0
    for axis_at, parts in shards:
        heights = jax.random.uniform(jax.random.fold_in(jax.random.fold_in(stream_key, 6), axis_at), (parts,), jnp.float32, low / len(shards), high / len(shards))
        factor_of = factor_of * jnp.repeat(jnp.exp(heights), shape[axis_at] // parts).reshape((-1,) + (1,) * (len(shape) - 1 - axis_at))
    return factor_of


def centred(key, dims, spread, reach, cuts=(), kind=jnp.bfloat16):
    entries = spread * jax.random.normal(key, dims, jnp.float32)
    if cuts:
        entries = entries * steps_of(key, dims, cuts, -0.22, 0.18)
    return jnp.clip(entries, -reach, reach).astype(kind)


def setup_inputs(seed: int = 0) -> dict:
    key_list = jax.random.split(jax.random.key(seed), 8)
    tile_rows = draw_tile_rows(jax.random.fold_in(key_list[7], 71), 0)
    tile_cols = draw_tile_cols(jax.random.fold_in(key_list[7], 71), 0)
    tile_count = draw_tile_count(jax.random.fold_in(key_list[7], 71), 0)
    tile_vals = centred(key_list[3], (USER_BLOCKS, ITEM_BLOCKS, TILES_DEV, TILE, TILE), 1.0, 6.0, ((0, 32), (1, 4)))
    user_degree = draw_user_degree(jax.random.fold_in(key_list[7], 71), 0)
    item_degree = draw_item_degree(jax.random.fold_in(key_list[7], 71), 0)
    start_items = centred(key_list[6], (K, ITEMS), 1.0, 6.0, ((1, 128),))
    return {"tile_rows": tile_rows, "tile_cols": tile_cols, "tile_count": tile_count, "tile_vals": tile_vals, "user_degree": user_degree, "item_degree": item_degree, "start_items": start_items}


def orthonormalize(raw, total):
    gram = jnp.einsum('kr,jr->kj', raw.astype(jnp.float32), raw.astype(jnp.float32), precision=lax.Precision.HIGHEST, preferred_element_type=jnp.float32) / total
    lower = jnp.linalg.cholesky(gram)
    return lax.linalg.triangular_solve(lower, raw, left_side=True, lower=True)

def user_side(sent_items, tile_rows, tile_cols, tile_count, tile_vals):
    blocks = sent_items.reshape(K, ITEM_BLOCKS, IT, TILE)

    def one_user_block(user_block):

        def add_item(total, item_block):
            values = tile_vals[user_block, item_block].astype(jnp.float32)
            rows = tile_rows[user_block, item_block]
            cols = tile_cols[user_block, item_block]
            live = (jnp.arange(TILES_DEV) < tile_count[user_block, item_block]).astype(jnp.float32)
            picked = jnp.take(blocks[:, item_block], cols, axis=1).astype(jnp.float32)
            product = jnp.einsum('ktc,trc->ktr', picked, values, precision=lax.Precision.HIGHEST)
            product = product * live[None, :, None]
            return (total.at[:, rows, :].add(product), None)
        total, _ = lax.scan(add_item, jnp.zeros((K, UT, TILE), jnp.float32), jnp.arange(ITEM_BLOCKS))
        return total
    result = lax.map(one_user_block, jnp.arange(USER_BLOCKS))
    return result.transpose(1, 0, 2, 3).reshape(K, USERS)

def item_side(sent_users, tile_rows, tile_cols, tile_count, tile_vals):
    blocks = sent_users.reshape(K, USER_BLOCKS, UT, TILE)

    def one_item_block(item_block):

        def add_user(total, user_block):
            values = tile_vals[user_block, item_block].astype(jnp.float32)
            rows = tile_rows[user_block, item_block]
            cols = tile_cols[user_block, item_block]
            live = (jnp.arange(TILES_DEV) < tile_count[user_block, item_block]).astype(jnp.float32)
            picked = jnp.take(blocks[:, user_block], rows, axis=1).astype(jnp.float32)
            product = jnp.einsum('ktr,trc->ktc', picked, values, precision=lax.Precision.HIGHEST)
            product = product * live[None, :, None]
            return (total.at[:, cols, :].add(product), None)
        total, _ = lax.scan(add_user, jnp.zeros((K, IT, TILE), jnp.float32), jnp.arange(USER_BLOCKS))
        return total
    result = lax.map(one_item_block, jnp.arange(ITEM_BLOCKS))
    return result.transpose(1, 0, 2, 3).reshape(K, ITEMS)

def reference(tile_rows, tile_cols, tile_count, tile_vals, user_degree, item_degree, start_items):
    user_scale = lax.rsqrt(user_degree.astype(jnp.float32))
    item_scale = lax.rsqrt(item_degree.astype(jnp.float32))
    panel = start_items.astype(jnp.float32)
    user_panel = jnp.zeros((K, USERS), jnp.float32)
    for step in range(ITERS):
        sent_items = item_scale[None, :] * panel
        user_raw = user_scale[None, :] * user_side(sent_items, tile_rows, tile_cols, tile_count, tile_vals)
        user_panel = orthonormalize(user_raw, USERS)
        sent_users = user_scale[None, :] * user_panel
        item_raw = item_scale[None, :] * item_side(sent_users, tile_rows, tile_cols, tile_count, tile_vals)
        panel = orthonormalize(item_raw, ITEMS)
    return (user_panel, panel)
```

```python
import functools

import jax
import jax.numpy as jnp
from jax import lax
from jax.experimental import pallas as pl
from jax.experimental.pallas import tpu as pltpu
from jax.sharding import PartitionSpec as P

K = 64
H = K // 2
Q = K // 4
TILE = 128
UT = 64
IT = 64
CHUNK = 64
UNROLL = 8
NCH = 4
MESH = pl.DeviceIdType.MESH
F32 = jnp.float32
HIGHEST = lax.Precision.HIGHEST
VMEM_LIMIT = 56 * 1024 * 1024
VMEM = pl.BlockSpec(memory_space=pltpu.VMEM)


def tile_products(contract, count_s, from_s, to_s, full_ref, vals_ref, out_ref, split):
    g = pl.program_id(0)

    @pl.when(g == 0)
    def _():
        def prepare(i, carry):
            x = full_ref[i]
            high = x.astype(jnp.bfloat16)
            split[i, :K] = high
            split[i, K:] = (x - high.astype(F32)).astype(jnp.bfloat16)
            out_ref[i] = jnp.zeros((K, TILE), F32)
            return carry

        lax.fori_loop(0, IT, prepare, 0)

    count = count_s[0]
    live = jnp.clip(count - g * CHUNK, 0, CHUNK)

    def group(j, carry):
        base = j * UNROLL
        products = []
        for q in range(UNROLL):
            both = lax.dot_general(
                split[from_s[g * CHUNK + base + q]],
                vals_ref[base + q],
                (((1,), (contract,)), ((), ())),
                preferred_element_type=F32,
            )
            products.append(jnp.where(base + q < live, both[:K] + both[K:], 0.0))
        for q in range(UNROLL):
            to = to_s[g * CHUNK + base + q]
            out_ref[to] = out_ref[to] + products[q]
        return carry

    lax.fori_loop(0, (live + UNROLL - 1) // UNROLL, group, 0)


def products_call(contract, count, source, target, full, vals):
    slots = vals.shape[0]
    whole = pl.BlockSpec((UT, K, TILE), lambda g, n, a, b: (0, 0, 0))
    return pl.pallas_call(
        functools.partial(tile_products, contract),
        out_shape=jax.ShapeDtypeStruct((UT, K, TILE), F32),
        grid_spec=pltpu.PrefetchScalarGridSpec(
            num_scalar_prefetch=3,
            grid=(slots // CHUNK,),
            in_specs=[
                whole,
                pl.BlockSpec(
                    (CHUNK, TILE, TILE),
                    lambda g, n, a, b: (jnp.minimum(g, (n[0] - 1) // CHUNK), 0, 0),
                ),
            ],
            out_specs=whole,
            scratch_shapes=[pltpu.VMEM((UT, 2 * K, TILE), jnp.bfloat16)],
        ),
        compiler_params=pltpu.CompilerParams(vmem_limit_bytes=VMEM_LIMIT),
        name="products_users" if contract == 1 else "products_items",
    )(count, source, target, full, vals)


class Place:
    def __init__(self):
        users = lax.axis_index("users")
        items = lax.axis_index("items")
        self.xh, self.y, self.z = users // 16, (users // 4) % 4, users % 4
        self.xl, self.core = items // 2, items % 2

    def at(self, xh=None, y=None, z=None, xl=None, core=None):
        xh = self.xh if xh is None else xh
        y = self.y if y is None else y
        z = self.z if z is None else z
        xl = self.xl if xl is None else xl
        core = self.core if core is None else core
        return ((xh * 4 + y) * 4 + z, xl * 2 + core)

    def near(self):
        out = []
        for k in range(1, 8):
            j = (self.xh * 4 + self.xl * 2 + self.core + k) % 8
            out.append(self.at(xh=j // 4, xl=(j // 2) % 2, core=j % 2))
        return out

    def plane(self):
        out = []
        for k in range(1, 16):
            j = (self.y * 4 + self.z + k) % 16
            out.append(self.at(y=j // 4, z=j % 4))
        return out


def greet(devices):
    barrier = pltpu.get_barrier_semaphore()
    for device in devices:
        pl.semaphore_signal(barrier, inc=1, device_id=device, device_id_type=MESH)
    pl.semaphore_wait(barrier, len(devices))


class Sems:
    def __init__(self, send, recv):
        self.send, self.recv, self.used = send, recv, 0

    def copy(self, src, dst, device):
        k = self.used
        self.used += 1
        return pltpu.make_async_remote_copy(
            src_ref=src,
            dst_ref=dst,
            send_sem=self.send.at[k],
            recv_sem=self.recv.at[k],
            device_id=device,
            device_id_type=MESH,
        )


LOW, HIGH = slice(0, Q), slice(Q, H)


def rows(half, part=None):
    start = half * H + (Q if part is HIGH else 0)
    return pl.ds(start, H if part is None else Q)


class RingGather:
    def __init__(self, sems, slab, me, device):
        plus, minus, far = (me + 1) % 4, (me + 3) % 4, (me + 2) % 4
        to_plus, to_minus = device(plus), device(minus)
        self.own = [
            sems.copy(slab(me, None), slab(me, None), to_plus),
            sems.copy(slab(me, None), slab(me, None), to_minus),
        ]
        self.on = [
            sems.copy(slab(minus, LOW), slab(minus, LOW), to_plus),
            sems.copy(slab(plus, HIGH), slab(plus, HIGH), to_minus),
        ]
        del far

    def start(self):
        for copy in self.own:
            copy.start()

    def forward(self):
        for own, on in zip(self.own, self.on):
            own.wait_recv()
            on.start()

    def finish(self):
        for on in self.on:
            on.wait_recv()

    def drain(self):
        for copy in self.own + self.on:
            copy.wait_send()


class RingReduce:
    def __init__(self, sems, slab, me, device, first, second, sums):
        plus, minus, far = (me + 1) % 4, (me + 3) % 4, (me + 2) % 4
        to_plus, to_minus = device(plus), device(minus)
        self.slab, self.me, self.plus, self.minus = slab, me, plus, minus
        self.first, self.second, self.sums = first, second, sums
        self.far = [
            sems.copy(slab(far, LOW), first.at[0], to_plus),
            sems.copy(slab(far, HIGH), first.at[1], to_minus),
        ]
        self.plain = [
            sems.copy(slab(plus, HIGH), second.at[0, 1], to_plus),
            sems.copy(slab(minus, LOW), second.at[1, 0], to_minus),
        ]
        self.summed = [
            sems.copy(sums.at[0], second.at[0, 0], to_plus),
            sems.copy(sums.at[1], second.at[1, 1], to_minus),
        ]

    def start(self):
        for copy in self.far + self.plain:
            copy.start()

    def forward(self):
        for k, (place, part) in enumerate(((self.plus, LOW), (self.minus, HIGH))):
            self.far[k].wait_recv()
            self.sums[k] = self.slab(place, part)[...] + self.first[k]
            self.summed[k].start()

    def finish(self, out_low, out_high):
        self.plain[1].wait_recv()
        self.summed[0].wait_recv()
        out_low[...] = self.slab(self.me, LOW)[...] + (self.second[0, 0] + self.second[1, 0])
        self.plain[0].wait_recv()
        self.summed[1].wait_recv()
        out_high[...] = self.slab(self.me, HIGH)[...] + (self.second[0, 1] + self.second[1, 1])

    def drain(self):
        for copy in self.far + self.plain + self.summed:
            copy.wait_send()


class GramSum:
    def __init__(self, sems, place, near_buf, plane_buf):
        self.near_buf, self.plane_buf = near_buf, plane_buf
        self.n = place.xh * 4 + place.xl * 2 + place.core
        self.p = place.y * 4 + place.z
        self.near = [sems.copy(near_buf.at[self.n], near_buf.at[self.n], d) for d in place.near()]
        self.plane = [sems.copy(plane_buf.at[self.p], plane_buf.at[self.p], d) for d in place.plane()]

    def start(self, value):
        self.near_buf[self.n] = value
        for copy in self.near:
            copy.start()

    def forward(self):
        for copy in self.near:
            copy.wait_recv()
        total = self.near_buf[0]
        for k in range(1, 8):
            total = total + self.near_buf[k]
        self.plane_buf[self.p] = total
        for copy in self.plane:
            copy.start()

    def finish(self):
        for copy in self.plane:
            copy.wait_recv()
        total = self.plane_buf[0]
        for k in range(1, 16):
            total = total + self.plane_buf[k]
        return total

    def drain(self):
        for copy in self.near + self.plane:
            copy.wait_send()


def inverse_factor(gram):
    row = lax.broadcasted_iota(jnp.int32, (K, 2 * K), 0)
    lane = lax.broadcasted_iota(jnp.int32, (K, 2 * K), 1)
    work = jnp.concatenate([gram, jnp.zeros((K, K), F32)], axis=1)
    work = work + jnp.where(lane == row + K, 1.0, 0.0)
    for j in range(K):
        scale = lax.rsqrt(work[j : j + 1, j : j + 1])
        pivot = work[j : j + 1, :] * scale
        column = work[:, j : j + 1] * scale
        work = jnp.where(row > j, work - column * pivot, jnp.where(row == j, pivot, work))
    return work[:, K:]


def apply(left, right):
    return jnp.dot(left, right, precision=HIGHEST, preferred_element_type=F32)


def gram_of(tiles):
    total = jnp.zeros((K, K), F32)
    for x in tiles:
        total = total + lax.dot_general(
            x, x, (((1,), (1,)), ((), ())), precision=HIGHEST, preferred_element_type=F32
        )
    return total


def gather_rings(sems, place, full):
    def along_y(half, whole):
        if whole:
            slab = lambda n, part: full.at[:, n, :, :, rows(half, part)]
        else:
            slab = lambda n, part: full.at[:, n, place.z, :, rows(half, part)]
        return RingGather(sems, slab, place.y, lambda n: place.at(y=n))

    def along_z(half, whole):
        if whole:
            slab = lambda n, part: full.at[:, :, n, :, rows(half, part)]
        else:
            slab = lambda n, part: full.at[:, place.y, n, :, rows(half, part)]
        return RingGather(sems, slab, place.z, lambda n: place.at(z=n))

    return [along_y(0, False), along_z(1, False)], [along_z(0, True), along_y(1, True)]


def across_x(sems, place, full):
    own = full.at[place.xh, place.y, place.z]
    return sems.copy(own, own, place.at(xh=1 - place.xh))


def gather_kernel(sent_ref, full, send, recv):
    place = Place()
    sems = Sems(send, recv)
    cross = across_x(sems, place, full)
    first, second = gather_rings(sems, place, full)
    greet(
        [place.at(xh=1 - place.xh)]
        + [place.at(y=(place.y + k) % 4) for k in (1, 3)]
        + [place.at(z=(place.z + k) % 4) for k in (1, 3)]
    )
    full[place.xh, place.y, place.z] = sent_ref[...]
    cross.start()
    cross.wait_recv()
    for step in ("start", "forward"):
        for ring in first:
            getattr(ring, step)()
    for ring, later in zip(first, second):
        ring.finish()
        later.start()
    for step in ("forward", "finish"):
        for ring in second:
            getattr(ring, step)()
    cross.wait_send()
    for ring in first + second:
        ring.drain()


def remote_call(kernel, name, collective_id, out_shape, scratch_shapes, copies, *args):
    return pl.pallas_call(
        kernel,
        out_shape=out_shape,
        in_specs=[VMEM] * len(args),
        out_specs=jax.tree.map(lambda _: VMEM, out_shape),
        scratch_shapes=[
            *scratch_shapes,
            pltpu.SemaphoreType.DMA((copies,)),
            pltpu.SemaphoreType.DMA((copies,)),
        ],
        compiler_params=pltpu.CompilerParams(
            collective_id=collective_id, has_side_effects=True, vmem_limit_bytes=VMEM_LIMIT
        ),
        name=name,
    )(*args)


FULL = (2, 4, 4, 2, K, TILE)


def gather_call(sent):
    return remote_call(
        gather_kernel, "items_gather", 1, jax.ShapeDtypeStruct(FULL, F32), [], 17, sent
    )


def reduce_scratch():
    out = []
    for lead in ((2, 4, 2), (2, 4, 2), (2, 2), (2, 2)):
        out += [
            pltpu.VMEM((2, *lead, Q, TILE), F32),
            pltpu.VMEM((2, 2, *lead, Q, TILE), F32),
            pltpu.VMEM((2, *lead, Q, TILE), F32),
        ]
    return out + [
        pltpu.VMEM((2, 4, 2, H, TILE), F32),
        pltpu.VMEM((2, 4, 2, H, TILE), F32),
        pltpu.VMEM((2, 2, K, TILE), F32),
        pltpu.VMEM((2, K, TILE), F32),
    ]


REDUCE_SCRATCH = 16


def reduce_rings(sems, place, partial, bufs):
    half0, half1, mine, arrived = bufs[12:16]
    part = lambda p: slice(0, H) if p is None else p
    first = [
        RingReduce(sems, lambda n, p: partial.at[:, :, n, :, rows(0, p)], place.z,
                   lambda n: place.at(z=n), *bufs[0:3]),
        RingReduce(sems, lambda n, p: partial.at[:, n, :, :, rows(1, p)], place.y,
                   lambda n: place.at(y=n), *bufs[3:6]),
    ]
    second = [
        RingReduce(sems, lambda n, p: half0.at[:, n, :, part(p)], place.y,
                   lambda n: place.at(y=n), *bufs[6:9]),
        RingReduce(sems, lambda n, p: half1.at[:, n, :, part(p)], place.z,
                   lambda n: place.at(z=n), *bufs[9:12]),
    ]
    outs = [
        [half0.at[:, :, :, LOW], half0.at[:, :, :, HIGH]],
        [half1.at[:, :, :, LOW], half1.at[:, :, :, HIGH]],
        [mine.at[:, :, rows(0, LOW)], mine.at[:, :, rows(0, HIGH)]],
        [mine.at[:, :, rows(1, LOW)], mine.at[:, :, rows(1, HIGH)]],
    ]
    cross = sems.copy(mine.at[1 - place.xh], arrived, place.at(xh=1 - place.xh))
    return first, second, outs, cross, mine, arrived


def reduced(place, first, second, outs, cross, mine, arrived, gram):
    for ring in first:
        ring.start()
    for ring in first:
        ring.forward()
    gram.forward()
    for ring, later, out in zip(first, second, outs):
        ring.finish(*out)
        later.start()
    for ring in second:
        ring.forward()
    total = gram.finish()
    for ring, out in zip(second, outs[2:]):
        ring.finish(*out)
    cross.start()
    return total


def middle_kernel(user_total, item_total, partial, gram_ref, scale_ref, full, factor_ref, *scratch):
    bufs, (near1, plane1, near2, plane2, send, recv) = scratch[:REDUCE_SCRATCH], scratch[REDUCE_SCRATCH:]
    place = Place()
    sems = Sems(send, recv)
    first, second, outs, cross, mine, arrived = reduce_rings(sems, place, partial, bufs)
    gram1 = GramSum(sems, place, near1, plane1)
    gram2 = GramSum(sems, place, near2, plane2)
    spread = across_x(sems, place, full)
    gather1, gather2 = gather_rings(sems, place, full)
    greet(place.near() + place.plane())

    gram1.start(gram_ref[...])
    total = reduced(place, first, second, outs, cross, mine, arrived, gram1)
    inverse = inverse_factor(total / user_total)
    cross.wait_recv()
    raw = [
        apply(inverse, scale_ref[t : t + 1] * (mine[place.xh, t] + arrived[t])) for t in range(2)
    ]
    for t in range(2):
        full[place.xh, place.y, place.z, t] = scale_ref[t : t + 1] * raw[t]
    spread.start()
    gram2.start(gram_of(raw))
    spread.wait_recv()
    for ring in gather1:
        ring.start()
    gram2.forward()
    for ring in gather1:
        ring.forward()
    for ring, later in zip(gather1, gather2):
        ring.finish()
        later.start()
    for ring in gather2:
        ring.forward()
    factor_ref[...] = inverse_factor(gram2.finish() / item_total)
    for ring in gather2:
        ring.finish()
    cross.wait_send()
    spread.wait_send()
    for part in first + second + gather1 + gather2 + [gram1, gram2]:
        part.drain()


GRAM_SCRATCH = [pltpu.VMEM((8, K, K), F32), pltpu.VMEM((16, K, K), F32)]


def middle_call(user_total, item_total, partial, gram, scale):
    return remote_call(
        functools.partial(middle_kernel, user_total, item_total),
        "items_reduce_gather",
        2,
        (jax.ShapeDtypeStruct(FULL, F32), jax.ShapeDtypeStruct((K, K), F32)),
        reduce_scratch() + GRAM_SCRATCH * 2,
        24 + 1 + 44 + 17,
        partial,
        gram,
        scale,
    )


def last_kernel(
    user_total, item_total, partial, gram_ref, scale_ref, factor_ref, users_ref, user_out, item_out, *scratch
):
    bufs, (near1, plane1, near2, plane2, send, recv) = scratch[:REDUCE_SCRATCH], scratch[REDUCE_SCRATCH:]
    place = Place()
    sems = Sems(send, recv)
    first, second, outs, cross, mine, arrived = reduce_rings(sems, place, partial, bufs)
    gram1 = GramSum(sems, place, near1, plane1)
    gram2 = GramSum(sems, place, near2, plane2)
    greet(place.near() + place.plane())

    gram1.start(gram_ref[...])
    total = reduced(place, first, second, outs, cross, mine, arrived, gram1)
    inverse = inverse_factor(total / user_total)
    cross.wait_recv()
    raw = [
        apply(inverse, apply(factor_ref[...], scale_ref[t : t + 1] * (mine[place.xh, t] + arrived[t])))
        for t in range(2)
    ]
    gram2.start(gram_of(raw))
    for t in range(8):
        user_out[:, t * TILE : (t + 1) * TILE] = apply(inverse, users_ref[t])
    gram2.forward()
    for t in range(8, 16):
        user_out[:, t * TILE : (t + 1) * TILE] = apply(inverse, users_ref[t])
    inverse2 = inverse_factor(gram2.finish() / item_total)
    for t in range(2):
        item_out[:, t * TILE : (t + 1) * TILE] = apply(inverse2, raw[t])
    cross.wait_send()
    for part in first + second + [gram1, gram2]:
        part.drain()


def last_call(user_total, item_total, partial, gram, scale, factor, users):
    return remote_call(
        functools.partial(last_kernel, user_total, item_total),
        "items_reduce_last",
        3,
        (jax.ShapeDtypeStruct((K, 16 * TILE), F32), jax.ShapeDtypeStruct((K, 2 * TILE), F32)),
        reduce_scratch() + GRAM_SCRATCH * 2,
        24 + 1 + 44,
        partial,
        gram,
        scale,
        factor,
        users,
    )


def users_kernel(with_factor, *refs):
    if with_factor:
        partial, scale_ref, factor_ref, *refs = refs
    else:
        partial, scale_ref, *refs = refs
    full, raw_ref, gram_ref, from_core, from_chip, sums, send, recv = refs
    place = Place()
    sems = Sems(send, recv)
    xl, core = place.xl, place.core
    size = 16 // NCH
    sibling = place.at(core=1 - core)
    partner = place.at(xl=1 - xl)

    def tiles(xq, cq, j):
        return pl.ds((xq * 2 + cq) * 16 + j * size, size)

    def to_core(xq, slot):
        return [
            sems.copy(partial.at[tiles(xq, 1 - core, j)], from_core.at[slot, j], sibling) for j in range(NCH)
        ]

    core_other, core_mine = to_core(1 - xl, 0), to_core(xl, 1)
    to_chip = [sems.copy(sums.at[j], from_chip.at[j], partner) for j in range(NCH)]
    mine = [full.at[tiles(xl, core, j)] for j in range(NCH)]
    theirs = [full.at[tiles(1 - xl, core, j)] for j in range(NCH)]
    done_chip = [sems.copy(mine[j], mine[j], partner) for j in range(NCH)]
    done_core = [sems.copy(mine[j], mine[j], sibling) for j in range(NCH)]
    passed = [sems.copy(theirs[j], theirs[j], sibling) for j in range(NCH)]
    greet([sibling, partner])

    for copy in core_other + core_mine:
        copy.start()
    for j in range(NCH):
        core_other[j].wait_recv()
        sums[j] = partial[tiles(1 - xl, core, j)] + from_core[0, j]
        to_chip[j].start()
    for j in range(NCH):
        core_mine[j].wait_recv()
        to_chip[j].wait_recv()
        for t in range(size):
            row = j * size + t
            scale = scale_ref[row : row + 1]
            place_t = (xl * 2 + core) * 16 + row
            raw = scale * (partial[place_t] + (from_core[1, j, t] + from_chip[j, t]))
            full[place_t] = scale * raw
            raw_ref[row] = raw
        done_chip[j].start()
        done_core[j].start()
    if with_factor:
        for t in range(16):
            raw_ref[t] = apply(factor_ref[...], raw_ref[t])
    gram_ref[...] = gram_of([raw_ref[t] for t in range(16)])
    for j in range(NCH):
        done_chip[j].wait_recv()
        passed[j].start()
    for j in range(NCH):
        done_core[j].wait_recv()
        passed[j].wait_recv()
    for copy in core_other + core_mine + to_chip + done_chip + done_core + passed:
        copy.wait_send()


def users_call(partial, scale, factor=None):
    size = 16 // NCH
    return remote_call(
        functools.partial(users_kernel, factor is not None),
        "users_sum" if factor is None else "users_sum_again",
        4 if factor is None else 5,
        (
            jax.ShapeDtypeStruct((UT, K, TILE), F32),
            jax.ShapeDtypeStruct((16, K, TILE), F32),
            jax.ShapeDtypeStruct((K, K), F32),
        ),
        [
            pltpu.VMEM((2, NCH, size, K, TILE), F32),
            pltpu.VMEM((NCH, size, K, TILE), F32),
            pltpu.VMEM((NCH, size, K, TILE), F32),
        ],
        6 * NCH,
        partial,
        scale,
        *([] if factor is None else [factor]),
    )


def body(tile_rows, tile_cols, tile_count, tile_vals, user_degree, item_degree, start_items):
    tile_row, tile_col, count = tile_rows[0, 0], tile_cols[0, 0], tile_count[0]
    vals = tile_vals[0, 0]
    user_scale = lax.rsqrt(user_degree.astype(F32)).reshape(16, TILE)
    item_scale = lax.rsqrt(item_degree.astype(F32)).reshape(2, TILE)
    user_total = 16 * TILE * lax.axis_size("users") * lax.axis_size("items")
    item_total = 2 * TILE * lax.axis_size("users") * lax.axis_size("items")
    sent = item_scale[:, None, :] * start_items.astype(F32).reshape(K, 2, TILE).transpose(1, 0, 2)

    full_items = gather_call(sent)
    partial = products_call(1, count, tile_col, tile_row, full_items.reshape(IT, K, TILE), vals)
    full_users, _, gram = users_call(partial, user_scale)
    partial = products_call(0, count, tile_row, tile_col, full_users, vals)
    full_items, factor = middle_call(user_total, item_total, partial.reshape(FULL), gram, item_scale)
    partial = products_call(1, count, tile_col, tile_row, full_items.reshape(IT, K, TILE), vals)
    full_users, raw, gram = users_call(partial, user_scale, factor)
    partial = products_call(0, count, tile_row, tile_col, full_users, vals)
    return last_call(user_total, item_total, partial.reshape(FULL), gram, item_scale, factor, raw)


def solution(mesh):
    in_specs = (
        P("users", "items", None),
        P("users", "items", None),
        P("users", "items"),
        P("users", "items", None, None, None),
        P(("users", "items")),
        P(("items", "users")),
        P(None, ("items", "users")),
    )
    out_specs = (P(None, ("users", "items")), P(None, ("items", "users")))
    return jax.shard_map(body, mesh=mesh, in_specs=in_specs, out_specs=out_specs, check_vma=False)
```

```python
import functools

import jax
import jax.numpy as jnp
from jax import lax
from jax.experimental import pallas as pl
from jax.experimental.pallas import tpu as pltpu
from jax.sharding import PartitionSpec as P

K = 64
H = K // 2
Q = K // 4
TILE = 128
UT = 64
IT = 64
CHUNK = 64
UNROLL = 64
NCH = 8
MESH = pl.DeviceIdType.MESH
F32 = jnp.float32
HIGHEST = lax.Precision.HIGHEST
VMEM_LIMIT = 56 * 1024 * 1024
VMEM = pl.BlockSpec(memory_space=pltpu.VMEM)


def tile_products(contract, count_s, from_s, to_s, full_ref, vals_ref, out_ref, split):
    g = pl.program_id(0)

    @pl.when(g == 0)
    def _():
        def prepare(j, carry):
            for q in range(4):
                x = full_ref[j * 4 + q]
                high = x.astype(jnp.bfloat16)
                split[j * 4 + q, :K] = high
                split[j * 4 + q, K:] = (x - high.astype(F32)).astype(jnp.bfloat16)
                out_ref[j * 4 + q] = jnp.zeros((K, TILE), F32)
            return carry

        lax.fori_loop(0, IT // 4, prepare, 0)

    count = count_s[0]
    live = jnp.clip(count - g * CHUNK, 0, CHUNK)

    def group(j, carry):
        base = j * UNROLL
        for q in range(UNROLL):
            both = lax.dot_general(
                split[from_s[g * CHUNK + base + q]],
                vals_ref[base + q],
                (((1,), (contract,)), ((), ())),
                preferred_element_type=F32,
            )
            to = to_s[g * CHUNK + base + q]
            out_ref[to] = out_ref[to] + jnp.where(base + q < live, both[:K] + both[K:], 0.0)
        return carry

    lax.fori_loop(0, (live + UNROLL - 1) // UNROLL, group, 0)


def products_call(contract, count, source, target, full, vals):
    slots = vals.shape[0]
    whole = pl.BlockSpec((UT, K, TILE), lambda g, n, a, b: (0, 0, 0))
    return pl.pallas_call(
        functools.partial(tile_products, contract),
        out_shape=jax.ShapeDtypeStruct((UT, K, TILE), F32),
        grid_spec=pltpu.PrefetchScalarGridSpec(
            num_scalar_prefetch=3,
            grid=(slots // CHUNK,),
            in_specs=[
                whole,
                pl.BlockSpec(
                    (CHUNK, TILE, TILE),
                    lambda g, n, a, b: (jnp.minimum(g, (n[0] - 1) // CHUNK), 0, 0),
                ),
            ],
            out_specs=whole,
            scratch_shapes=[pltpu.VMEM((UT, 2 * K, TILE), jnp.bfloat16)],
        ),
        compiler_params=pltpu.CompilerParams(vmem_limit_bytes=VMEM_LIMIT),
        name="products_users" if contract == 1 else "products_items",
    )(count, source, target, full, vals)


class Place:
    def __init__(self):
        users = lax.axis_index("users")
        items = lax.axis_index("items")
        self.xh, self.y, self.z = users // 16, (users // 4) % 4, users % 4
        self.xl, self.core = items // 2, items % 2

    def at(self, xh=None, y=None, z=None, xl=None, core=None):
        xh = self.xh if xh is None else xh
        y = self.y if y is None else y
        z = self.z if z is None else z
        xl = self.xl if xl is None else xl
        core = self.core if core is None else core
        return ((xh * 4 + y) * 4 + z, xl * 2 + core)

    def near(self):
        out = []
        for k in range(1, 8):
            j = (self.xh * 4 + self.xl * 2 + self.core + k) % 8
            out.append(self.at(xh=j // 4, xl=(j // 2) % 2, core=j % 2))
        return out

    def plane(self):
        out = []
        for k in range(1, 16):
            j = (self.y * 4 + self.z + k) % 16
            out.append(self.at(y=j // 4, z=j % 4))
        return out


def greet(devices):
    barrier = pltpu.get_barrier_semaphore()
    for device in devices:
        pl.semaphore_signal(barrier, inc=1, device_id=device, device_id_type=MESH)
    pl.semaphore_wait(barrier, len(devices))


class Sems:
    def __init__(self, send, recv):
        self.send, self.recv, self.used = send, recv, 0

    def copy(self, src, dst, device):
        k = self.used
        self.used += 1
        return pltpu.make_async_remote_copy(
            src_ref=src,
            dst_ref=dst,
            send_sem=self.send.at[k],
            recv_sem=self.recv.at[k],
            device_id=device,
            device_id_type=MESH,
        )


LOW, HIGH = slice(0, Q), slice(Q, H)


def rows(half, part=None):
    start = half * H + (Q if part is HIGH else 0)
    return pl.ds(start, H if part is None else Q)


class RingGather:
    def __init__(self, sems, slab, me, device):
        plus, minus, far = (me + 1) % 4, (me + 3) % 4, (me + 2) % 4
        to_plus, to_minus = device(plus), device(minus)
        self.own = [
            sems.copy(slab(me, None), slab(me, None), to_plus),
            sems.copy(slab(me, None), slab(me, None), to_minus),
        ]
        self.on = [
            sems.copy(slab(minus, LOW), slab(minus, LOW), to_plus),
            sems.copy(slab(plus, HIGH), slab(plus, HIGH), to_minus),
        ]
        del far

    def start(self):
        for copy in self.own:
            copy.start()

    def forward(self):
        for own, on in zip(self.own, self.on):
            own.wait_recv()
            on.start()

    def finish(self):
        for on in self.on:
            on.wait_recv()

    def drain(self):
        for copy in self.own + self.on:
            copy.wait_send()


class RingReduce:
    def __init__(self, sems, slab, me, device, first, second, sums):
        plus, minus, far = (me + 1) % 4, (me + 3) % 4, (me + 2) % 4
        to_plus, to_minus = device(plus), device(minus)
        self.slab, self.me, self.plus, self.minus = slab, me, plus, minus
        self.first, self.second, self.sums = first, second, sums
        self.far = [
            sems.copy(slab(far, LOW), first.at[0], to_plus),
            sems.copy(slab(far, HIGH), first.at[1], to_minus),
        ]
        self.plain = [
            sems.copy(slab(plus, HIGH), second.at[0, 1], to_plus),
            sems.copy(slab(minus, LOW), second.at[1, 0], to_minus),
        ]
        self.summed = [
            sems.copy(sums.at[0], second.at[0, 0], to_plus),
            sems.copy(sums.at[1], second.at[1, 1], to_minus),
        ]

    def start_far(self):
        for copy in self.far:
            copy.start()

    def start_plain(self):
        for copy in self.plain:
            copy.start()

    def forward(self):
        for k, (place, part) in enumerate(((self.plus, LOW), (self.minus, HIGH))):
            self.far[k].wait_recv()
            self.sums[k] = self.slab(place, part)[...] + self.first[k]
            self.summed[k].start()

    def finish(self, out_low, out_high):
        self.plain[1].wait_recv()
        self.summed[0].wait_recv()
        out_low[...] = self.slab(self.me, LOW)[...] + (self.second[0, 0] + self.second[1, 0])
        self.plain[0].wait_recv()
        self.summed[1].wait_recv()
        out_high[...] = self.slab(self.me, HIGH)[...] + (self.second[0, 1] + self.second[1, 1])

    def drain(self):
        for copy in self.far + self.plain + self.summed:
            copy.wait_send()


class GroupSum:
    def __init__(self, sems, buf, index, others):
        self.buf, self.index = buf, index
        self.copies = [sems.copy(buf.at[index], buf.at[index], d) for d in others]

    def start(self, value):
        self.buf[self.index] = value
        for copy in self.copies:
            copy.start()

    def finish(self):
        for copy in self.copies:
            copy.wait_recv()
        total = self.buf[0]
        for k in range(1, self.buf.shape[0]):
            total = total + self.buf[k]
        return total

    def drain(self):
        for copy in self.copies:
            copy.wait_send()


def near_sum(sems, place, buf):
    return GroupSum(sems, buf, place.xh * 4 + place.xl * 2 + place.core, place.near())


def plane_sum(sems, place, buf):
    return GroupSum(sems, buf, place.y * 4 + place.z, place.plane())


NEAR_BUF = pltpu.VMEM((8, K, K), F32)
PLANE_BUF = pltpu.VMEM((16, K, K), F32)


class Factor:
    def __init__(self, gram):
        self.row = lax.broadcasted_iota(jnp.int32, (K, 2 * K), 0)
        self.lane = lax.broadcasted_iota(jnp.int32, (K, 2 * K), 1)
        work = jnp.concatenate([gram, jnp.zeros((K, K), F32)], axis=1)
        self.work = work + jnp.where(self.lane == self.row + K, 1.0, 0.0)

    def columns(self, start, stop, step=8):
        work = self.work
        for j in range(start, stop, step):
            cols = [jnp.broadcast_to(work[:, k : k + 1], (K, 2 * K)) for k in range(j, j + step)]
            for s in range(step):
                k = j + s
                factor = jnp.where(self.row > k, cols[s] * (1.0 / cols[s][k : k + 1]), 0.0)
                for m in range(s + 1, step):
                    cols[m] = cols[m] - factor * cols[m][k : k + 1]
                work = work - factor * work[k : k + 1]
        self.work = work

    def inverse(self):
        pivots = jnp.sum(jnp.where(self.lane == self.row, self.work, 0.0), axis=1, keepdims=True)
        return self.work[:, K:] * lax.rsqrt(pivots)


def apply(left, right):
    return jnp.dot(left, right, precision=HIGHEST, preferred_element_type=F32)


def gram_of(tiles):
    total = jnp.zeros((K, K), F32)
    for x in tiles:
        total = total + lax.dot_general(
            x, x, (((1,), (1,)), ((), ())), precision=HIGHEST, preferred_element_type=F32
        )
    return total


class Spread:
    def __init__(self, sems, place, full):
        at_y, at_z = (lambda n: place.at(y=n)), (lambda n: place.at(z=n))
        y, z = place.y, place.z
        self.first = [
            RingGather(sems, lambda n, p: full.at[:, n, z, :, rows(0, p)], y, at_y),
            RingGather(sems, lambda n, p: full.at[:, y, n, :, rows(1, p)], z, at_z),
        ]
        order = lambda n: [n, (n + 3) % 4, (n + 1) % 4, (n + 2) % 4]
        self.second = [
            [RingGather(sems, lambda n, p, m=m: full.at[:, m, n, :, rows(0, p)], z, at_z) for m in order(y)],
            [RingGather(sems, lambda n, p, m=m: full.at[:, n, m, :, rows(1, p)], y, at_y) for m in order(z)],
        ]

    def start(self):
        for ring in self.first:
            ring.start()
        for rings in self.second:
            rings[0].start()

    def forward(self):
        for k in range(2):
            for ring, rings in zip(self.first, self.second):
                ring.own[k].wait_recv()
                ring.on[k].start()
                rings[1 + k].start()

    def turn(self):
        for rings in self.second:
            rings[0].forward()
        for ring, rings in zip(self.first, self.second):
            ring.finish()
            rings[3].start()

    def last(self):
        for k in (1, 2, 3):
            for rings in self.second:
                rings[k].forward()

    def finish(self):
        for k in range(4):
            for rings in self.second:
                rings[k].finish()

    def drain(self):
        for ring in self.first + self.second[0] + self.second[1]:
            ring.drain()


SPREAD_COPIES = 40


def across_x(sems, place, full):
    own = full.at[place.xh, place.y, place.z]
    return sems.copy(own, own, place.at(xh=1 - place.xh))


def gather_kernel(sent_ref, full, send, recv):
    place = Place()
    sems = Sems(send, recv)
    cross = across_x(sems, place, full)
    spread = Spread(sems, place, full)
    greet(
        [place.at(xh=1 - place.xh)]
        + [place.at(y=(place.y + k) % 4) for k in (1, 3)]
        + [place.at(z=(place.z + k) % 4) for k in (1, 3)]
    )
    full[place.xh, place.y, place.z] = sent_ref[...]
    cross.start()
    cross.wait_recv()
    spread.start()
    spread.forward()
    spread.turn()
    spread.last()
    spread.finish()
    cross.wait_send()
    spread.drain()


def remote_call(kernel, name, collective_id, out_shape, scratch_shapes, copies, *args):
    return pl.pallas_call(
        kernel,
        out_shape=out_shape,
        in_specs=[VMEM] * len(args),
        out_specs=jax.tree.map(lambda _: VMEM, out_shape),
        scratch_shapes=[
            *scratch_shapes,
            pltpu.SemaphoreType.DMA((copies,)),
            pltpu.SemaphoreType.DMA((copies,)),
        ],
        compiler_params=pltpu.CompilerParams(
            collective_id=collective_id, has_side_effects=True, vmem_limit_bytes=VMEM_LIMIT
        ),
        name=name,
    )(*args)


FULL = (2, 4, 4, 2, K, TILE)


def gather_call(sent):
    return remote_call(
        gather_kernel, "items_gather", 1, jax.ShapeDtypeStruct(FULL, F32), [], 1 + SPREAD_COPIES, sent
    )


def ring_bufs(lead):
    return [
        pltpu.VMEM((2, *lead, Q, TILE), F32),
        pltpu.VMEM((2, 2, *lead, Q, TILE), F32),
        pltpu.VMEM((2, *lead, Q, TILE), F32),
    ]


REDUCE_SCRATCH = (
    ring_bufs((2, 4, 2, 2))
    + ring_bufs((2, 2))
    + ring_bufs((2, 2))
    + [
        pltpu.VMEM((2, 2, 4, 2, H, TILE), F32),
        pltpu.VMEM((2, 2, K, TILE), F32),
        pltpu.VMEM((2, K, TILE), F32),
    ]
)
REDUCE_COPIES = 60 + 1


class Reduce:
    def __init__(self, sems, place, partial, bufs):
        a1, a2, a3, b1, b2, b3, c1, c2, c3, kept, mine, arrived = bufs
        at_y, at_z = (lambda n: place.at(y=n)), (lambda n: place.at(z=n))
        y, z = place.y, place.z
        self.place, self.mine, self.arrived = place, mine, arrived
        order = lambda n: [(n + 2) % 4, (n + 1) % 4, (n + 3) % 4, n]
        part = lambda p: slice(0, H) if p is None else p
        view = lambda ref, h, k: ref.at[:, h, k]
        view2 = lambda ref, h, k: ref.at[:, :, h, k]
        slab0 = lambda m: lambda n, p: partial.at[:, m, n, :, rows(0, p)]
        slab1 = lambda m: lambda n, p: partial.at[:, n, m, :, rows(1, p)]
        self.first = [
            [RingReduce(sems, slab0(m), z, at_z, view(a1, 0, k), view2(a2, 0, k), view(a3, 0, k))
             for k, m in enumerate(order(y))],
            [RingReduce(sems, slab1(m), y, at_y, view(a1, 1, k), view2(a2, 1, k), view(a3, 1, k))
             for k, m in enumerate(order(z))],
        ]
        self.outs = [
            [[kept.at[h, :, m, :, LOW], kept.at[h, :, m, :, HIGH]] for m in order(n)] for h, n in ((0, y), (1, z))
        ]
        self.second = [
            RingReduce(sems, lambda n, p: kept.at[0, :, n, :, part(p)], y, at_y, b1, b2, b3),
            RingReduce(sems, lambda n, p: kept.at[1, :, n, :, part(p)], z, at_z, c1, c2, c3),
        ]
        self.cross = sems.copy(mine.at[1 - place.xh], arrived, place.at(xh=1 - place.xh))

    def start(self):
        for k in range(4):
            for rings in self.first:
                rings[k].start_far()
        for k in range(4):
            for rings in self.first:
                rings[k].start_plain()

    def forward(self):
        for k in range(4):
            for rings in self.first:
                rings[k].forward()

    def turn(self):
        for rings, out, later in zip(self.first, self.outs, self.second):
            rings[0].finish(*out[0])
            later.start_far()

    def middle(self):
        for k in (1, 2):
            for rings, out in zip(self.first, self.outs):
                rings[k].finish(*out[k])
        for later in self.second:
            later.start_plain()
            later.forward()

    def last(self):
        for rings, out in zip(self.first, self.outs):
            rings[3].finish(*out[3])
        for half, later in enumerate(self.second):
            later.finish(self.mine.at[:, :, rows(half, LOW)], self.mine.at[:, :, rows(half, HIGH)])
        self.cross.start()

    def finish(self):
        self.cross.wait_recv()

    def total(self, t):
        return self.mine[self.place.xh, t] + self.arrived[t]

    def drain(self):
        for ring in self.first[0] + self.first[1] + self.second:
            ring.drain()
        self.cross.wait_send()


def reduced(reduce, near, plane_ref, user_total):
    near.start(plane_ref[...])
    reduce.start()
    reduce.forward()
    factor = Factor(near.finish() / user_total)
    factor.columns(0, K // 2)
    reduce.turn()
    reduce.middle()
    factor.columns(K // 2, K)
    inverse = factor.inverse()
    reduce.last()
    return inverse


def middle_kernel(user_total, partial, plane_ref, scale_ref, full, near_ref, *scratch):
    *bufs, near1, near2, send, recv = scratch
    place = Place()
    sems = Sems(send, recv)
    reduce = Reduce(sems, place, partial, bufs)
    gram1, gram2 = near_sum(sems, place, near1), near_sum(sems, place, near2)
    cross = across_x(sems, place, full)
    spread = Spread(sems, place, full)
    greet(place.near() + place.plane())

    inverse = reduced(reduce, gram1, plane_ref, user_total)
    reduce.finish()
    raw = [apply(inverse, scale_ref[t : t + 1] * reduce.total(t)) for t in range(2)]
    for t in range(2):
        full[place.xh, place.y, place.z, t] = scale_ref[t : t + 1] * raw[t]
    cross.start()
    gram2.start(gram_of(raw))
    cross.wait_recv()
    spread.start()
    spread.forward()
    spread.turn()
    spread.last()
    near_ref[...] = gram2.finish()
    spread.finish()
    cross.wait_send()
    for part in (reduce, spread, gram1, gram2):
        part.drain()


def middle_call(user_total, partial, plane, scale):
    return remote_call(
        functools.partial(middle_kernel, user_total),
        "items_reduce_gather",
        2,
        (jax.ShapeDtypeStruct(FULL, F32), jax.ShapeDtypeStruct((K, K), F32)),
        [*REDUCE_SCRATCH, NEAR_BUF, NEAR_BUF],
        REDUCE_COPIES + 14 + 1 + SPREAD_COPIES,
        partial,
        plane,
        scale,
    )


def last_kernel(
    user_total, item_total, partial, plane_ref, scale_ref, factor_ref, users_ref, user_out, item_out, *scratch
):
    *bufs, near1, near2, plane2, send, recv = scratch
    place = Place()
    sems = Sems(send, recv)
    reduce = Reduce(sems, place, partial, bufs)
    gram1, gram2 = near_sum(sems, place, near1), near_sum(sems, place, near2)
    gram2_plane = plane_sum(sems, place, plane2)
    greet(place.near() + place.plane())

    inverse = reduced(reduce, gram1, plane_ref, user_total)
    reduce.finish()
    raw = [apply(inverse, apply(factor_ref[...], scale_ref[t : t + 1] * reduce.total(t))) for t in range(2)]
    gram2.start(gram_of(raw))
    for t in range(8):
        user_out[:, t * TILE : (t + 1) * TILE] = apply(inverse, users_ref[t])
    gram2_plane.start(gram2.finish())
    for t in range(8, 16):
        user_out[:, t * TILE : (t + 1) * TILE] = apply(inverse, users_ref[t])
    factor = Factor(gram2_plane.finish() / item_total)
    factor.columns(0, K)
    inverse2 = factor.inverse()
    for t in range(2):
        item_out[:, t * TILE : (t + 1) * TILE] = apply(inverse2, raw[t])
    for part in (reduce, gram1, gram2, gram2_plane):
        part.drain()


def last_call(user_total, item_total, partial, plane, scale, factor, users):
    return remote_call(
        functools.partial(last_kernel, user_total, item_total),
        "items_reduce_last",
        3,
        (jax.ShapeDtypeStruct((K, 16 * TILE), F32), jax.ShapeDtypeStruct((K, 2 * TILE), F32)),
        [*REDUCE_SCRATCH, NEAR_BUF, NEAR_BUF, PLANE_BUF],
        REDUCE_COPIES + 14 + 15,
        partial,
        plane,
        scale,
        factor,
        users,
    )


def users_kernel(item_total, *refs):
    again = item_total is not None
    if again:
        partial, scale_ref, near_ref, full, raw_ref, plane_ref, factor_ref, *refs = refs
        item_plane, *refs = refs
    else:
        partial, scale_ref, full, raw_ref, plane_ref, *refs = refs
    from_core, from_chip, sums, user_plane, send, recv = refs
    place = Place()
    sems = Sems(send, recv)
    xl, core = place.xl, place.core
    size = 16 // NCH
    sibling = place.at(core=1 - core)
    partner = place.at(xl=1 - xl)

    def tiles(xq, cq, j):
        return pl.ds((xq * 2 + cq) * 16 + j * size, size)

    def to_core(xq, slot):
        return [
            sems.copy(partial.at[tiles(xq, 1 - core, j)], from_core.at[slot, j], sibling) for j in range(NCH)
        ]

    core_other, core_mine = to_core(1 - xl, 0), to_core(xl, 1)
    to_chip = [sems.copy(sums.at[j], from_chip.at[j], partner) for j in range(NCH)]
    mine = [full.at[tiles(xl, core, j)] for j in range(NCH)]
    theirs = [full.at[tiles(1 - xl, core, j)] for j in range(NCH)]
    done_chip = [sems.copy(mine[j], mine[j], partner) for j in range(NCH)]
    done_core = [sems.copy(mine[j], mine[j], sibling) for j in range(NCH)]
    passed = [sems.copy(theirs[j], theirs[j], sibling) for j in range(NCH)]
    gram = plane_sum(sems, place, user_plane)
    if again:
        item_gram = plane_sum(sems, place, item_plane)
    greet([sibling, partner] + place.plane())

    for copy in core_other + core_mine:
        copy.start()
    if again:
        item_gram.start(near_ref[...])
    for j in range(NCH):
        core_other[j].wait_recv()
        sums[j] = partial[tiles(1 - xl, core, j)] + from_core[0, j]
        to_chip[j].start()
    if again:
        factor = Factor(item_gram.finish() / item_total)
        factor.columns(0, K)
        factor_ref[...] = factor.inverse()
    for j in range(NCH):
        core_mine[j].wait_recv()
        to_chip[j].wait_recv()
        for t in range(size):
            row = j * size + t
            scale = scale_ref[row : row + 1]
            place_t = (xl * 2 + core) * 16 + row
            raw = scale * (partial[place_t] + (from_core[1, j, t] + from_chip[j, t]))
            full[place_t] = scale * raw
            raw_ref[row] = raw
        done_chip[j].start()
        done_core[j].start()
    if again:
        for t in range(16):
            raw_ref[t] = apply(factor_ref[...], raw_ref[t])
    gram.start(gram_of([raw_ref[t] for t in range(16)]))
    for j in range(NCH):
        done_chip[j].wait_recv()
        passed[j].start()
    for j in range(NCH):
        done_core[j].wait_recv()
        passed[j].wait_recv()
    plane_ref[...] = gram.finish()
    for copy in core_other + core_mine + to_chip + done_chip + done_core + passed:
        copy.wait_send()
    gram.drain()
    if again:
        item_gram.drain()


def users_call(partial, scale, near=None, item_total=None):
    size = 16 // NCH
    square = jax.ShapeDtypeStruct((K, K), F32)
    again = near is not None
    return remote_call(
        functools.partial(users_kernel, item_total),
        "users_sum_again" if again else "users_sum",
        5 if again else 4,
        (
            jax.ShapeDtypeStruct((UT, K, TILE), F32),
            jax.ShapeDtypeStruct((16, K, TILE), F32),
            *([square] * (2 if again else 1)),
        ),
        [
            *([PLANE_BUF] if again else []),
            pltpu.VMEM((2, NCH, size, K, TILE), F32),
            pltpu.VMEM((NCH, size, K, TILE), F32),
            pltpu.VMEM((NCH, size, K, TILE), F32),
            PLANE_BUF,
        ],
        7 * NCH + 30,
        partial,
        scale,
        *([near] if again else []),
    )


def body(tile_rows, tile_cols, tile_count, tile_vals, user_degree, item_degree, start_items):
    tile_row, tile_col, count = tile_rows[0, 0], tile_cols[0, 0], tile_count[0]
    vals = tile_vals[0, 0]
    user_scale = lax.rsqrt(user_degree.astype(F32)).reshape(16, TILE)
    item_scale = lax.rsqrt(item_degree.astype(F32)).reshape(2, TILE)
    user_total = 16 * TILE * lax.axis_size("users") * lax.axis_size("items")
    item_total = 2 * TILE * lax.axis_size("users") * lax.axis_size("items")
    sent = item_scale[:, None, :] * start_items.astype(F32).reshape(K, 2, TILE).transpose(1, 0, 2)

    full_items = gather_call(sent)
    partial = products_call(1, count, tile_col, tile_row, full_items.reshape(IT, K, TILE), vals)
    full_users, _, plane = users_call(partial, user_scale)
    partial = products_call(0, count, tile_row, tile_col, full_users, vals)
    full_items, near = middle_call(user_total, partial.reshape(FULL), plane, item_scale)
    partial = products_call(1, count, tile_col, tile_row, full_items.reshape(IT, K, TILE), vals)
    full_users, raw, plane, factor = users_call(partial, user_scale, near, item_total)
    partial = products_call(0, count, tile_row, tile_col, full_users, vals)
    return last_call(user_total, item_total, partial.reshape(FULL), plane, item_scale, factor, raw)


def solution(mesh):
    in_specs = (
        P("users", "items", None),
        P("users", "items", None),
        P("users", "items"),
        P("users", "items", None, None, None),
        P(("users", "items")),
        P(("items", "users")),
        P(None, ("items", "users")),
    )
    out_specs = (P(None, ("users", "items")), P(None, ("items", "users")))
    return jax.shard_map(body, mesh=mesh, in_specs=in_specs, out_specs=out_specs, check_vma=False)
```

```python
import functools

import jax
import jax.numpy as jnp
from jax import lax
from jax.experimental import pallas as pl
from jax.experimental.pallas import tpu as pltpu
from jax.sharding import PartitionSpec as P

K = 64
KH = K // 2
H = KH // 2
Q = KH // 4
TILE = 128
UT = 64
IT = 64
ITERS = 2
UNROLL = 64
LOADS = 4
NCH = 2
SIZE = 16 // NCH
MESH = pl.DeviceIdType.MESH
F32 = jnp.float32
HIGHEST = lax.Precision.HIGHEST
VMEM_LIMIT = 63 * 1024 * 1024
VMEM = pl.BlockSpec(memory_space=pltpu.VMEM)
SMEM = pl.BlockSpec(memory_space=pltpu.SMEM)


class Place:
    def __init__(self):
        users = lax.axis_index("users")
        items = lax.axis_index("items")
        self.xh, self.y, self.z = users // 16, (users // 4) % 4, users % 4
        self.xl, self.core = items // 2, items % 2

    def at(self, xh=None, y=None, z=None, xl=None, core=None):
        xh = self.xh if xh is None else xh
        y = self.y if y is None else y
        z = self.z if z is None else z
        xl = self.xl if xl is None else xl
        core = self.core if core is None else core
        return ((xh * 4 + y) * 4 + z, xl * 2 + core)

    def near(self):
        out = []
        for k in range(1, 8):
            j = (self.xh * 4 + self.xl * 2 + self.core + k) % 8
            out.append(self.at(xh=j // 4, xl=(j // 2) % 2, core=j % 2))
        return out

    def plane(self):
        out = []
        for k in range(1, 16):
            j = (self.y * 4 + self.z + k) % 16
            out.append(self.at(y=j // 4, z=j % 4))
        return out


def greet(devices):
    barrier = pltpu.get_barrier_semaphore()
    for device in devices:
        pl.semaphore_signal(barrier, inc=1, device_id=device, device_id_type=MESH)
    pl.semaphore_wait(barrier, len(devices))


class Sems:
    def __init__(self, send, recv):
        self.send, self.recv, self.used = send, recv, 0

    def copy(self, src, dst, device):
        k = self.used
        self.used += 1
        return pltpu.make_async_remote_copy(
            src_ref=src,
            dst_ref=dst,
            send_sem=self.send.at[k],
            recv_sem=self.recv.at[k],
            device_id=device,
            device_id_type=MESH,
        )


LOW, HIGH = slice(0, Q), slice(Q, H)


def rows(way, part=None):
    start = way * H + (Q if part is HIGH else 0)
    return pl.ds(start, H if part is None else Q)


class RingGather:
    def __init__(self, sems, slab, me, device):
        plus, minus, far = (me + 1) % 4, (me + 3) % 4, (me + 2) % 4
        to_plus, to_minus = device(plus), device(minus)
        self.own = [
            sems.copy(slab(me, None), slab(me, None), to_plus),
            sems.copy(slab(me, None), slab(me, None), to_minus),
        ]
        self.on = [
            sems.copy(slab(minus, LOW), slab(minus, LOW), to_plus),
            sems.copy(slab(plus, HIGH), slab(plus, HIGH), to_minus),
        ]
        del far

    def start(self):
        for copy in self.own:
            copy.start()

    def forward(self):
        for own, on in zip(self.own, self.on):
            own.wait_recv()
            on.start()

    def finish(self):
        for on in self.on:
            on.wait_recv()

    def drain(self):
        for copy in self.own + self.on:
            copy.wait_send()


class RingReduce:
    def __init__(self, sems, slab, me, device, first, second, sums):
        plus, minus, far = (me + 1) % 4, (me + 3) % 4, (me + 2) % 4
        to_plus, to_minus = device(plus), device(minus)
        self.slab, self.me, self.plus, self.minus = slab, me, plus, minus
        self.first, self.second, self.sums = first, second, sums
        self.far = [
            sems.copy(slab(far, LOW), first.at[0], to_plus),
            sems.copy(slab(far, HIGH), first.at[1], to_minus),
        ]
        self.plain = [
            sems.copy(slab(plus, HIGH), second.at[0, 1], to_plus),
            sems.copy(slab(minus, LOW), second.at[1, 0], to_minus),
        ]
        self.summed = [
            sems.copy(sums.at[0], second.at[0, 0], to_plus),
            sems.copy(sums.at[1], second.at[1, 1], to_minus),
        ]

    def start(self):
        for copy in self.far + self.plain:
            copy.start()

    def forward(self):
        for k, (place, part) in enumerate(((self.plus, LOW), (self.minus, HIGH))):
            self.far[k].wait_recv()
            self.sums[k] = self.slab(place, part)[...] + self.first[k]
            self.summed[k].start()

    def finish(self, out_low, out_high):
        self.plain[1].wait_recv()
        self.summed[0].wait_recv()
        out_low[...] = self.slab(self.me, LOW)[...] + (self.second[0, 0] + self.second[1, 0])
        self.plain[0].wait_recv()
        self.summed[1].wait_recv()
        out_high[...] = self.slab(self.me, HIGH)[...] + (self.second[0, 1] + self.second[1, 1])

    def drain(self):
        for copy in self.far + self.plain + self.summed:
            copy.wait_send()


class GroupSum:
    def __init__(self, sems, buf, index, others):
        self.buf, self.index = buf, index
        self.copies = [sems.copy(buf.at[index], buf.at[index], d) for d in others]

    def start(self, value):
        self.buf[self.index] = value
        for copy in self.copies:
            copy.start()

    def finish(self):
        for copy in self.copies:
            copy.wait_recv()
        total = self.buf[0]
        for k in range(1, self.buf.shape[0]):
            total = total + self.buf[k]
        return total

    def drain(self):
        for copy in self.copies:
            copy.wait_send()


def near_sum(sems, place, buf):
    return GroupSum(sems, buf, place.xh * 4 + place.xl * 2 + place.core, place.near())


def plane_sum(sems, place, buf):
    return GroupSum(sems, buf, place.y * 4 + place.z, place.plane())


class Factor:
    def __init__(self, gram):
        self.row = lax.broadcasted_iota(jnp.int32, (K, 2 * K), 0)
        self.lane = lax.broadcasted_iota(jnp.int32, (K, 2 * K), 1)
        work = jnp.concatenate([gram, jnp.zeros((K, K), F32)], axis=1)
        self.work = work + jnp.where(self.lane == self.row + K, 1.0, 0.0)

    def columns(self, start, stop, step=8):
        work = self.work
        for j in range(start, stop, step):
            cols = [jnp.broadcast_to(work[:, k : k + 1], (K, 2 * K)) for k in range(j, j + step)]
            for s in range(step):
                k = j + s
                factor = jnp.where(self.row > k, cols[s] * (1.0 / cols[s][k : k + 1]), 0.0)
                for m in range(s + 1, step):
                    cols[m] = cols[m] - factor * cols[m][k : k + 1]
                work = work - factor * work[k : k + 1]
        self.work = work

    def inverse(self):
        pivots = jnp.sum(jnp.where(self.lane == self.row, self.work, 0.0), axis=1, keepdims=True)
        return self.work[:, K:] * lax.rsqrt(pivots)


def apply(left, right):
    return jnp.dot(left, right, precision=HIGHEST, preferred_element_type=F32)


def gram_of(tiles):
    total = jnp.zeros((K, K), F32)
    for x in tiles:
        total = total + lax.dot_general(
            x, x, (((1,), (1,)), ((), ())), precision=HIGHEST, preferred_element_type=F32
        )
    return total


class Spread:
    def __init__(self, sems, place, full):
        at_y, at_z = (lambda n: place.at(y=n)), (lambda n: place.at(z=n))
        y, z = place.y, place.z
        self.first = [
            RingGather(sems, lambda n, p: full.at[:, n, z, :, rows(0, p)], y, at_y),
            RingGather(sems, lambda n, p: full.at[:, y, n, :, rows(1, p)], z, at_z),
        ]
        self.second = [
            RingGather(sems, lambda n, p: full.at[:, :, n, :, rows(0, p)], z, at_z),
            RingGather(sems, lambda n, p: full.at[:, n, :, :, rows(1, p)], y, at_y),
        ]

    def start(self):
        for ring in self.first:
            ring.start()

    def forward(self):
        for ring in self.first:
            ring.forward()

    def turn(self):
        for ring, later in zip(self.first, self.second):
            ring.finish()
            later.start()

    def last(self):
        for ring in self.second:
            ring.forward()

    def finish(self):
        for ring in self.second:
            ring.finish()

    def drain(self):
        for ring in self.first + self.second:
            ring.drain()


SPREAD_COPIES = 16


def ring_bufs(lead):
    return [
        pltpu.VMEM((2, *lead, Q, TILE), F32),
        pltpu.VMEM((2, 2, *lead, Q, TILE), F32),
        pltpu.VMEM((2, *lead, Q, TILE), F32),
    ]


def reduce_bufs():
    return (
        ring_bufs((2, 4, 2))
        + ring_bufs((2, 4, 2))
        + ring_bufs((2, 2))
        + ring_bufs((2, 2))
        + [
            pltpu.VMEM((2, 4, 2, H, TILE), F32),
            pltpu.VMEM((2, 4, 2, H, TILE), F32),
            pltpu.VMEM((2, 2, KH, TILE), F32),
            pltpu.VMEM((2, KH, TILE), F32),
        ]
    )


REDUCE_BUFS = 16
REDUCE_COPIES = 25


class Reduce:
    def __init__(self, sems, place, partial, bufs):
        at_y, at_z = (lambda n: place.at(y=n)), (lambda n: place.at(z=n))
        y, z = place.y, place.z
        way0, way1, mine, arrived = bufs[12:16]
        self.place, self.mine, self.arrived = place, mine, arrived
        part = lambda p: slice(0, H) if p is None else p
        self.first = [
            RingReduce(sems, lambda n, p: partial.at[:, :, n, :, rows(0, p)], z, at_z, *bufs[0:3]),
            RingReduce(sems, lambda n, p: partial.at[:, n, :, :, rows(1, p)], y, at_y, *bufs[3:6]),
        ]
        self.second = [
            RingReduce(sems, lambda n, p: way0.at[:, n, :, part(p)], y, at_y, *bufs[6:9]),
            RingReduce(sems, lambda n, p: way1.at[:, n, :, part(p)], z, at_z, *bufs[9:12]),
        ]
        self.outs = [[way.at[:, :, :, LOW], way.at[:, :, :, HIGH]] for way in (way0, way1)]
        self.cross = sems.copy(mine.at[1 - place.xh], arrived, place.at(xh=1 - place.xh))

    def start(self):
        for ring in self.first:
            ring.start()

    def forward(self):
        for ring in self.first:
            ring.forward()

    def turn(self):
        for ring, out, later in zip(self.first, self.outs, self.second):
            ring.finish(*out)
            later.start()

    def last(self):
        for ring in self.second:
            ring.forward()

    def across(self):
        for way, ring in enumerate(self.second):
            ring.finish(self.mine.at[:, :, rows(way, LOW)], self.mine.at[:, :, rows(way, HIGH)])
        self.cross.start()

    def finish(self):
        self.cross.wait_recv()

    def total(self, t):
        return self.mine[self.place.xh, t] + self.arrived[t]

    def drain(self):
        for ring in self.first + self.second:
            ring.drain()
        self.cross.wait_send()


class UserSum:
    def __init__(self, sems, place, half, partial, full, from_core, from_chip, sums):
        xl, core = place.xl, place.core
        sibling, partner = place.at(core=1 - core), place.at(xl=1 - xl)
        self.rows = slice(half * KH, (half + 1) * KH)
        self.place, self.partial, self.full = place, partial, full
        self.from_core, self.from_chip, self.sums = from_core, from_chip, sums
        tiles = self.tiles
        chunks = range(NCH)

        def to_core(xq, slot):
            return [sems.copy(partial.at[tiles(xq, 1 - core, j)], from_core.at[slot, j], sibling) for j in chunks]

        self.core_other, self.core_mine = to_core(1 - xl, 0), to_core(xl, 1)
        self.to_chip = [sems.copy(sums.at[j], from_chip.at[j], partner) for j in chunks]
        mine = [full.at[tiles(xl, core, j)] for j in chunks]
        theirs = [full.at[tiles(1 - xl, core, j)] for j in chunks]
        self.done_chip = [sems.copy(m, m, partner) for m in mine]
        self.done_core = [sems.copy(m, m, sibling) for m in mine]
        self.passed = [sems.copy(t, t, sibling) for t in theirs]

    def tiles(self, xq, cq, j):
        return pl.ds((xq * 2 + cq) * 16 + j * SIZE, SIZE)

    def start(self):
        for copy in self.core_other + self.core_mine:
            copy.start()

    def sum(self):
        place = self.place
        for j in range(NCH):
            self.core_other[j].wait_recv()
            self.sums[j] = self.partial[self.tiles(1 - place.xl, place.core, j)] + self.from_core[0, j]
            self.to_chip[j].start()

    def combine(self, j, scale_ref, raw_ref):
        place = self.place
        self.core_mine[j].wait_recv()
        self.to_chip[j].wait_recv()
        for t in range(SIZE):
            row = j * SIZE + t
            tile = (place.xl * 2 + place.core) * 16 + row
            scale = scale_ref[row : row + 1]
            raw = scale * (self.partial[tile] + (self.from_core[1, j, t] + self.from_chip[j, t]))
            self.full[tile] = scale * raw
            raw_ref[row, self.rows] = raw
        self.done_chip[j].start()
        self.done_core[j].start()

    def hand_on(self):
        for j in range(NCH):
            self.done_chip[j].wait_recv()
            self.passed[j].start()

    def finish(self):
        for j in range(NCH):
            self.done_core[j].wait_recv()
            self.passed[j].wait_recv()

    def drain(self):
        for copy in self.core_other + self.core_mine + self.to_chip + self.done_chip + self.done_core + self.passed:
            copy.wait_send()


USER_COPIES = 6 * NCH


def products(order_s, last_s, side, tiles, load, store, split, sums, steps):
    def prepare(j, carry):
        for q in range(4):
            x = load(j * 4 + q)
            high = x.astype(jnp.bfloat16)
            split[j * 4 + q, :KH] = high
            split[j * 4 + q, KH:] = (x - high.astype(F32)).astype(jnp.bfloat16)
        return carry

    lax.fori_loop(0, IT // 4, prepare, 0)

    def group(j, total):
        for q in range(UNROLL):
            p = j * UNROLL + q
            both = jnp.dot(
                split[order_s[side, 1, p]], tiles[order_s[side, 0, p]], preferred_element_type=F32
            )
            total = jnp.where(order_s[side, 2, p] == 1, 0.0, total) + (both[:KH] + both[KH:])
            sums[p] = total
        for at, step in steps.items():
            pl.when(j == at)(step)
        return total

    lax.fori_loop(0, sums.shape[0] // UNROLL, group, jnp.zeros((KH, TILE), F32))

    def collect(j, carry):
        for q in range(4):
            r = j * 4 + q
            store(r, jnp.where(last_s[side, 1, r] == 1, sums[last_s[side, 0, r]], 0.0))
        return carry

    lax.fori_loop(0, UT // 4, collect, 0)


def whole_kernel(user_total, item_total, order_s, last_s, sent_ref, user_scale, item_scale, vals_ref, *refs):
    user_out, item_out, vals, turned, split, sums, full_items, full_users, part_users, part_items, raw_users, *refs = refs
    from_core, from_chip, chip_sums, near1, near2, plane1, plane2, load_sem, *refs = refs
    send, recv = refs[-2:]
    place = Place()
    xh, y, z = place.xh, place.y, place.z
    sems = Sems(send, recv)
    own = full_items.at[:, xh, y, z]
    cross = sems.copy(own, own, place.at(xh=1 - xh))
    spread = [Spread(sems, place, full_items.at[h]) for h in range(2)]
    reduce = [
        Reduce(sems, place, part_items.at[h], refs[h * REDUCE_BUFS : (h + 1) * REDUCE_BUFS]) for h in range(2)
    ]
    user = [
        UserSum(sems, place, h, part_users.at[h], full_users.at[h], from_core.at[h], from_chip.at[h], chip_sums.at[h])
        for h in range(2)
    ]
    user_near, item_near = near_sum(sems, place, near1), near_sum(sems, place, near2)
    user_plane, item_plane = plane_sum(sems, place, plane1), plane_sum(sems, place, plane2)
    slots = vals.shape[0]
    portion = slots // LOADS
    loads = [
        pltpu.make_async_copy(
            vals_ref.at[pl.ds(k * portion, portion)], vals.at[pl.ds(k * portion, portion)], load_sem.at[k]
        )
        for k in range(LOADS)
    ]
    for load in loads:
        load.start()
    greet(place.near() + place.plane())

    def turn_tiles(k):
        loads[k].wait()

        def some(j, carry):
            for q in range(8):
                at = k * portion + j * 8 + q
                turned[at] = vals[at].T
            return carry

        lax.fori_loop(0, portion // 8, some, 0)

    def place_of(ref, half, tile):
        return ref.at[half, tile // 32, (tile // 8) % 4, (tile // 2) % 4, tile % 2]

    def to_users(half, steps):
        def store(r, value):
            part_users[half, r] = value

        products(
            order_s, last_s, 0, turned, lambda i: place_of(full_items, half, i)[...], store, split, sums, steps
        )

    def to_items(half, steps):
        def store(r, value):
            place_of(part_items, half, r)[...] = value

        products(order_s, last_s, 1, vals, lambda i: full_users[half, i], store, split, sums, steps)

    own[...] = sent_ref[...]
    item_factor = None
    for step in range(ITERS):
        cross.start()
        first = step == 0
        if first:
            turn_tiles(0)
        else:
            item_near.start(gram_of(raw_items))
        cross.wait_recv()
        spread[0].start()
        if first:
            turn_tiles(1)
        spread[0].forward()
        spread[1].start()
        if first:
            turn_tiles(2)
        spread[0].turn()
        spread[1].forward()
        if first:
            turn_tiles(3)
        spread[0].last()
        spread[1].turn()
        spread[0].finish()

        def second_half():
            spread[1].last()

        to_users(0, {2: second_half})
        user[0].start()
        spread[1].finish()
        if not first:
            item_plane.start(item_near.finish())
        to_users(1, {0: user[0].sum, 6: lambda: user[0].combine(0, user_scale, raw_users)})
        user[1].start()
        user[0].combine(1, user_scale, raw_users)
        user[1].sum()
        if not first:
            factor = Factor(item_plane.finish() / item_total)
            factor.columns(0, K)
            item_factor = factor.inverse()
        user[0].hand_on()
        user[0].finish()
        to_items(
            0,
            {
                3: lambda: user[1].combine(0, user_scale, raw_users),
                6: lambda: user[1].combine(1, user_scale, raw_users),
            },
        )
        cross.wait_send()
        for part in spread:
            part.drain()
        reduce[0].start()
        if not first:
            for t in range(16):
                raw_users[t] = apply(item_factor, raw_users[t])
        user_plane.start(gram_of([raw_users[t] for t in range(16)]))
        user[1].hand_on()
        user[1].finish()

        def gram_step():
            user_near.start(user_plane.finish())

        to_items(1, {1: reduce[0].forward, 3: gram_step, 5: reduce[0].turn})
        reduce[1].start()
        reduce[0].last()
        factor = Factor(user_near.finish() / user_total)
        factor.columns(0, K // 2)
        reduce[1].forward()
        reduce[0].across()
        factor.columns(K // 2, K)
        user_factor = factor.inverse()
        reduce[1].turn()
        reduce[1].last()
        if not first:
            for t in range(16):
                user_out[:, t * TILE : (t + 1) * TILE] = apply(user_factor, raw_users[t])
        reduce[1].across()
        reduce[0].finish()
        reduce[1].finish()
        raw_items = []
        for t in range(2):
            total = jnp.concatenate([reduce[0].total(t), reduce[1].total(t)], axis=0)
            raw = item_scale[t : t + 1] * total
            if not first:
                raw = apply(item_factor, raw)
            raw_items.append(apply(user_factor, raw))
        for part in (*user, *reduce, user_plane, user_near):
            part.drain()
        if first:
            for t in range(2):
                sent = item_scale[t : t + 1] * raw_items[t]
                for h in range(2):
                    full_items[h, xh, y, z, t] = sent[h * KH : (h + 1) * KH]
        else:
            item_plane.drain()
            item_near.drain()

    item_near.start(gram_of(raw_items))
    item_plane.start(item_near.finish())
    factor = Factor(item_plane.finish() / item_total)
    factor.columns(0, K)
    last_factor = factor.inverse()
    for t in range(2):
        item_out[:, t * TILE : (t + 1) * TILE] = apply(last_factor, raw_items[t])
    item_near.drain()
    item_plane.drain()


def whole_call(user_total, item_total, order, last, sent, user_scale, item_scale, vals):
    slots = vals.shape[0]
    copies = 1 + 2 * (SPREAD_COPIES + REDUCE_COPIES + USER_COPIES) + 44
    tiles = pltpu.VMEM((slots, TILE, TILE), jnp.bfloat16)
    full = (2, 2, 4, 4, 2, KH, TILE)
    scratch = [
        tiles,
        tiles,
        pltpu.VMEM((IT, 2 * KH, TILE), jnp.bfloat16),
        pltpu.VMEM((slots, KH, TILE), F32),
        pltpu.VMEM(full, F32),
        pltpu.VMEM((2, UT, KH, TILE), F32),
        pltpu.VMEM((2, UT, KH, TILE), F32),
        pltpu.VMEM(full, F32),
        pltpu.VMEM((16, K, TILE), F32),
        pltpu.VMEM((2, 2, NCH, SIZE, KH, TILE), F32),
        pltpu.VMEM((2, NCH, SIZE, KH, TILE), F32),
        pltpu.VMEM((2, NCH, SIZE, KH, TILE), F32),
        pltpu.VMEM((8, K, K), F32),
        pltpu.VMEM((8, K, K), F32),
        pltpu.VMEM((16, K, K), F32),
        pltpu.VMEM((16, K, K), F32),
        pltpu.SemaphoreType.DMA((LOADS,)),
        *reduce_bufs(),
        *reduce_bufs(),
        pltpu.SemaphoreType.DMA((copies,)),
        pltpu.SemaphoreType.DMA((copies,)),
    ]
    return pl.pallas_call(
        functools.partial(whole_kernel, user_total, item_total),
        out_shape=(
            jax.ShapeDtypeStruct((K, 16 * TILE), F32),
            jax.ShapeDtypeStruct((K, 2 * TILE), F32),
        ),
        in_specs=[SMEM, SMEM, VMEM, VMEM, VMEM, pl.BlockSpec(memory_space=pl.ANY)],
        out_specs=(VMEM, VMEM),
        scratch_shapes=scratch,
        compiler_params=pltpu.CompilerParams(
            collective_id=1, has_side_effects=True, vmem_limit_bytes=VMEM_LIMIT
        ),
        name="cocluster",
    )(order, last, sent, user_scale, item_scale, vals)


def slot_order(rows, cols, count):
    slots = rows.shape[0]
    at = jnp.arange(slots, dtype=jnp.int32)
    dead = jnp.where(at < count, 0, UT)
    target = jnp.stack([rows, cols]) + dead
    source = jnp.stack([cols, rows])
    code = (target * IT + source) * slots + at
    rank = jnp.sum((code[:, None, :] < code[:, :, None]).astype(jnp.int32), axis=2)
    ranked = jnp.sum(jnp.where(rank[:, None, :] == at[None, :, None], code[:, None, :], 0), axis=2)
    slot, source, target = ranked % slots, (ranked // slots) % IT, ranked // (slots * IT)
    before = jnp.concatenate([jnp.full((2, 1), -1, jnp.int32), target[:, :-1]], axis=1)
    order = jnp.stack([slot, source, (target != before).astype(jnp.int32)], axis=1)
    line = jnp.arange(UT, dtype=jnp.int32)[None, :, None]
    upto = jnp.sum((target[:, None, :] <= line).astype(jnp.int32), axis=2)
    has = jnp.sum((target[:, None, :] == line).astype(jnp.int32), axis=2)
    last = jnp.stack([jnp.maximum(upto - 1, 0), (has > 0).astype(jnp.int32)], axis=1)
    return order, last


def body(tile_rows, tile_cols, tile_count, tile_vals, user_degree, item_degree, start_items):
    user_scale = lax.rsqrt(user_degree.astype(F32)).reshape(16, TILE)
    item_scale = lax.rsqrt(item_degree.astype(F32)).reshape(2, TILE)
    user_total = 16 * TILE * lax.axis_size("users") * lax.axis_size("items")
    item_total = 2 * TILE * lax.axis_size("users") * lax.axis_size("items")
    start = start_items.astype(F32).reshape(2, KH, 2, TILE).transpose(0, 2, 1, 3)
    order, last = slot_order(tile_rows[0, 0], tile_cols[0, 0], tile_count[0, 0])
    return whole_call(
        user_total, item_total, order, last, item_scale[None, :, None, :] * start, user_scale, item_scale, tile_vals[0, 0]
    )


def solution(mesh):
    in_specs = (
        P("users", "items", None),
        P("users", "items", None),
        P("users", "items"),
        P("users", "items", None, None, None),
        P(("users", "items")),
        P(("items", "users")),
        P(None, ("items", "users")),
    )
    out_specs = (P(None, ("users", "items")), P(None, ("items", "users")))
    return jax.shard_map(body, mesh=mesh, in_specs=in_specs, out_specs=out_specs, check_vma=False)
```

```python
import functools

import jax
import jax.numpy as jnp
from jax import lax
from jax.experimental import pallas as pl
from jax.experimental.pallas import tpu as pltpu
from jax.sharding import PartitionSpec as P

K = 64
KH = K // 2
H = KH // 2
Q = KH // 4
TILE = 128
UT = 64
IT = 64
ITERS = 2
UNROLL = 64
LOADS = 4
NCH = 2
SIZE = 16 // NCH
MESH = pl.DeviceIdType.MESH
F32 = jnp.float32
HIGHEST = lax.Precision.HIGHEST
VMEM_LIMIT = 63 * 1024 * 1024
VMEM = pl.BlockSpec(memory_space=pltpu.VMEM)
SMEM = pl.BlockSpec(memory_space=pltpu.SMEM)


class Place:
    def __init__(self):
        users = lax.axis_index("users")
        items = lax.axis_index("items")
        self.xh, self.y, self.z = users // 16, (users // 4) % 4, users % 4
        self.xl, self.core = items // 2, items % 2

    def at(self, xh=None, y=None, z=None, xl=None, core=None):
        xh = self.xh if xh is None else xh
        y = self.y if y is None else y
        z = self.z if z is None else z
        xl = self.xl if xl is None else xl
        core = self.core if core is None else core
        return ((xh * 4 + y) * 4 + z, xl * 2 + core)

    def near(self):
        out = []
        for k in range(1, 8):
            j = (self.xh * 4 + self.xl * 2 + self.core + k) % 8
            out.append(self.at(xh=j // 4, xl=(j // 2) % 2, core=j % 2))
        return out

    def plane(self):
        out = []
        for k in range(1, 16):
            j = (self.y * 4 + self.z + k) % 16
            out.append(self.at(y=j // 4, z=j % 4))
        return out


def octet(place, along_y):
    line = place.y if along_y else place.z
    out = []
    for k in range(1, 8):
        j = (place.xh * 4 + line + k) % 8
        out.append((j // 4, j % 4, place.at(xh=j // 4, y=j % 4) if along_y else place.at(xh=j // 4, z=j % 4)))
    return out


def corners(place):
    out = []
    for k in range(1, 4):
        out.append(place.at(xh=1 - place.xh, y=(place.y + k) % 4))
        out.append(place.at(xh=1 - place.xh, z=(place.z + k) % 4))
    return out


def greet(devices):
    barrier = pltpu.get_barrier_semaphore()
    for device in devices:
        pl.semaphore_signal(barrier, inc=1, device_id=device, device_id_type=MESH)
    pl.semaphore_wait(barrier, len(devices))


class Sems:
    def __init__(self, send, recv):
        self.send, self.recv, self.used = send, recv, 0

    def copy(self, src, dst, device):
        k = self.used
        self.used += 1
        return pltpu.make_async_remote_copy(
            src_ref=src,
            dst_ref=dst,
            send_sem=self.send.at[k],
            recv_sem=self.recv.at[k],
            device_id=device,
            device_id_type=MESH,
        )


LOW, HIGH = slice(0, Q), slice(Q, H)


def rows(way, part=None):
    start = way * H + (Q if part is HIGH else 0)
    return pl.ds(start, H if part is None else Q)


class RingGather:
    def __init__(self, sems, slab, me, device):
        plus, minus, far = (me + 1) % 4, (me + 3) % 4, (me + 2) % 4
        to_plus, to_minus = device(plus), device(minus)
        self.own = [
            sems.copy(slab(me, None), slab(me, None), to_plus),
            sems.copy(slab(me, None), slab(me, None), to_minus),
        ]
        self.on = [
            sems.copy(slab(minus, LOW), slab(minus, LOW), to_plus),
            sems.copy(slab(plus, HIGH), slab(plus, HIGH), to_minus),
        ]
        del far

    def start(self):
        for copy in self.own:
            copy.start()

    def forward(self):
        for own, on in zip(self.own, self.on):
            own.wait_recv()
            on.start()

    def finish(self):
        for on in self.on:
            on.wait_recv()

    def drain(self):
        for copy in self.own + self.on:
            copy.wait_send()


class RingReduce:
    def __init__(self, sems, slab, me, device, first, second, sums):
        plus, minus, far = (me + 1) % 4, (me + 3) % 4, (me + 2) % 4
        to_plus, to_minus = device(plus), device(minus)
        self.slab, self.me, self.plus, self.minus = slab, me, plus, minus
        self.first, self.second, self.sums = first, second, sums
        self.far = [
            sems.copy(slab(far, LOW), first.at[0], to_plus),
            sems.copy(slab(far, HIGH), first.at[1], to_minus),
        ]
        self.plain = [
            sems.copy(slab(plus, HIGH), second.at[0, 1], to_plus),
            sems.copy(slab(minus, LOW), second.at[1, 0], to_minus),
        ]
        self.summed = [
            sems.copy(sums.at[0], second.at[0, 0], to_plus),
            sems.copy(sums.at[1], second.at[1, 1], to_minus),
        ]

    def start(self):
        for copy in self.far + self.plain:
            copy.start()

    def forward(self):
        for k, (place, part) in enumerate(((self.plus, LOW), (self.minus, HIGH))):
            self.far[k].wait_recv()
            self.sums[k] = self.slab(place, part)[...] + self.first[k]
            self.summed[k].start()

    def finish(self, out_low, out_high):
        self.plain[1].wait_recv()
        self.summed[0].wait_recv()
        out_low[...] = self.slab(self.me, LOW)[...] + (self.second[0, 0] + self.second[1, 0])
        self.plain[0].wait_recv()
        self.summed[1].wait_recv()
        out_high[...] = self.slab(self.me, HIGH)[...] + (self.second[0, 1] + self.second[1, 1])

    def drain(self):
        for copy in self.far + self.plain + self.summed:
            copy.wait_send()


class GroupSum:
    def __init__(self, sems, buf, index, others):
        self.buf, self.index = buf, index
        self.copies = [sems.copy(buf.at[index], buf.at[index], d) for d in others]

    def start(self, value):
        self.buf[self.index] = value
        for copy in self.copies:
            copy.start()

    def finish(self):
        for copy in self.copies:
            copy.wait_recv()
        total = self.buf[0]
        for k in range(1, self.buf.shape[0]):
            total = total + self.buf[k]
        return total

    def drain(self):
        for copy in self.copies:
            copy.wait_send()


def near_sum(sems, place, buf):
    return GroupSum(sems, buf, place.xh * 4 + place.xl * 2 + place.core, place.near())


def plane_sum(sems, place, buf):
    return GroupSum(sems, buf, place.y * 4 + place.z, place.plane())


class Factor:
    def __init__(self, gram):
        self.row = lax.broadcasted_iota(jnp.int32, (K, 2 * K), 0)
        self.lane = lax.broadcasted_iota(jnp.int32, (K, 2 * K), 1)
        work = jnp.concatenate([gram, jnp.zeros((K, K), F32)], axis=1)
        self.work = work + jnp.where(self.lane == self.row + K, 1.0, 0.0)

    def columns(self, start, stop, step=8):
        work = self.work
        for j in range(start, stop, step):
            cols = [jnp.broadcast_to(work[:, k : k + 1], (K, 2 * K)) for k in range(j, j + step)]
            for s in range(step):
                k = j + s
                factor = jnp.where(self.row > k, cols[s] * (1.0 / cols[s][k : k + 1]), 0.0)
                for m in range(s + 1, step):
                    cols[m] = cols[m] - factor * cols[m][k : k + 1]
                work = work - factor * work[k : k + 1]
        self.work = work

    def inverse(self):
        pivots = jnp.sum(jnp.where(self.lane == self.row, self.work, 0.0), axis=1, keepdims=True)
        return self.work[:, K:] * lax.rsqrt(pivots)


def apply(left, right):
    return jnp.dot(left, right, precision=HIGHEST, preferred_element_type=F32)


def gram_of(tiles):
    total = jnp.zeros((K, K), F32)
    for x in tiles:
        total = total + lax.dot_general(
            x, x, (((1,), (1,)), ((), ())), precision=HIGHEST, preferred_element_type=F32
        )
    return total


class Spread:
    def __init__(self, sems, place, full):
        at_y, at_z = (lambda n: place.at(y=n)), (lambda n: place.at(z=n))
        y, z = place.y, place.z
        self.direct = []
        for way in range(2):
            block = full.at[place.xh, y, z, :, rows(way)]
            self.direct += [sems.copy(block, block, device) for _, _, device in octet(place, way == 0)]
        self.rings = [
            RingGather(sems, lambda n, p: full.at[:, :, n, :, rows(0, p)], z, at_z),
            RingGather(sems, lambda n, p: full.at[:, n, :, :, rows(1, p)], y, at_y),
        ]

    def start(self):
        for copy in self.direct:
            copy.start()

    def turn(self):
        for way, ring in enumerate(self.rings):
            for copy in self.direct[way * 7 : way * 7 + 7]:
                copy.wait_recv()
            ring.start()

    def last(self):
        for ring in self.rings:
            ring.forward()

    def finish(self):
        for ring in self.rings:
            ring.finish()

    def drain(self):
        for copy in self.direct:
            copy.wait_send()
        for ring in self.rings:
            ring.drain()


SPREAD_COPIES = 22


def ring_bufs(lead):
    return [
        pltpu.VMEM((2, *lead, Q, TILE), F32),
        pltpu.VMEM((2, 2, *lead, Q, TILE), F32),
        pltpu.VMEM((2, *lead, Q, TILE), F32),
    ]


def reduce_bufs():
    return (
        ring_bufs((2, 4, 2))
        + ring_bufs((2, 4, 2))
        + [pltpu.VMEM((2, 2, 4, 2, H, TILE), F32), pltpu.VMEM((2, 7, 2, H, TILE), F32)]
    )


REDUCE_BUFS = 8
REDUCE_COPIES = 26


class Reduce:
    def __init__(self, sems, place, partial, bufs):
        at_y, at_z = (lambda n: place.at(y=n)), (lambda n: place.at(z=n))
        y, z = place.y, place.z
        self.ways, self.arrived = bufs[6:8]
        self.place = place
        self.rings = [
            RingReduce(sems, lambda n, p: partial.at[:, :, n, :, rows(0, p)], z, at_z, *bufs[0:3]),
            RingReduce(sems, lambda n, p: partial.at[:, n, :, :, rows(1, p)], y, at_y, *bufs[3:6]),
        ]
        self.direct = [
            [
                sems.copy(self.ways.at[way, xh, line], self.arrived.at[way, k], device)
                for k, (xh, line, device) in enumerate(octet(place, way == 0))
            ]
            for way in range(2)
        ]

    def start(self):
        for ring in self.rings:
            ring.start()

    def forward(self):
        for ring in self.rings:
            ring.forward()

    def turn(self):
        for way, ring in enumerate(self.rings):
            ring.finish(self.ways.at[way, :, :, :, LOW], self.ways.at[way, :, :, :, HIGH])
            for copy in self.direct[way]:
                copy.start()

    def finish(self):
        place = self.place
        sums = []
        for way, line in enumerate((place.y, place.z)):
            total = self.ways[way, place.xh, line]
            for k, copy in enumerate(self.direct[way]):
                copy.wait_recv()
                total = total + self.arrived[way, k]
            sums.append(total)
        return [jnp.concatenate([sums[0][t], sums[1][t]], axis=0) for t in range(2)]

    def drain(self):
        for ring in self.rings:
            ring.drain()
        for copy in self.direct[0] + self.direct[1]:
            copy.wait_send()


class UserSum:
    def __init__(self, sems, place, half, partial, full, from_core, from_chip, sums):
        xl, core = place.xl, place.core
        sibling, partner = place.at(core=1 - core), place.at(xl=1 - xl)
        self.rows = slice(half * KH, (half + 1) * KH)
        self.place, self.partial, self.full = place, partial, full
        self.from_core, self.from_chip, self.sums = from_core, from_chip, sums
        tiles = self.tiles
        chunks = range(NCH)

        def to_core(xq, slot):
            return [sems.copy(partial.at[tiles(xq, 1 - core, j)], from_core.at[slot, j], sibling) for j in chunks]

        self.core_other, self.core_mine = to_core(1 - xl, 0), to_core(xl, 1)
        self.to_chip = [sems.copy(sums.at[j], from_chip.at[j], partner) for j in chunks]
        mine = [full.at[tiles(xl, core, j)] for j in chunks]
        theirs = [full.at[tiles(1 - xl, core, j)] for j in chunks]
        self.done_chip = [sems.copy(m, m, partner) for m in mine]
        self.done_core = [sems.copy(m, m, sibling) for m in mine]
        self.passed = [sems.copy(t, t, sibling) for t in theirs]

    def tiles(self, xq, cq, j):
        return pl.ds((xq * 2 + cq) * 16 + j * SIZE, SIZE)

    def start(self):
        for copy in self.core_other + self.core_mine:
            copy.start()

    def sum(self):
        place = self.place
        for j in range(NCH):
            self.core_other[j].wait_recv()
            self.sums[j] = self.partial[self.tiles(1 - place.xl, place.core, j)] + self.from_core[0, j]
            self.to_chip[j].start()

    def combine(self, j, scale_ref, raw_ref):
        place = self.place
        self.core_mine[j].wait_recv()
        self.to_chip[j].wait_recv()
        for t in range(SIZE):
            row = j * SIZE + t
            tile = (place.xl * 2 + place.core) * 16 + row
            scale = scale_ref[row : row + 1]
            raw = scale * (self.partial[tile] + (self.from_core[1, j, t] + self.from_chip[j, t]))
            self.full[tile] = scale * raw
            raw_ref[row, self.rows] = raw
        self.done_chip[j].start()
        self.done_core[j].start()

    def hand_on(self):
        for j in range(NCH):
            self.done_chip[j].wait_recv()
            self.passed[j].start()

    def finish(self):
        for j in range(NCH):
            self.done_core[j].wait_recv()
            self.passed[j].wait_recv()

    def drain(self):
        for copy in self.core_other + self.core_mine + self.to_chip + self.done_chip + self.done_core + self.passed:
            copy.wait_send()


USER_COPIES = 6 * NCH


def products(order_s, last_s, side, tiles, load, store, split, sums, steps):
    def prepare(j, carry):
        for q in range(4):
            x = load(j * 4 + q)
            high = x.astype(jnp.bfloat16)
            split[j * 4 + q, :KH] = high
            split[j * 4 + q, KH:] = (x - high.astype(F32)).astype(jnp.bfloat16)
        return carry

    lax.fori_loop(0, IT // 4, prepare, 0)

    def group(j, total):
        for q in range(UNROLL):
            p = j * UNROLL + q
            both = jnp.dot(
                split[order_s[side, 1, p]], tiles[order_s[side, 0, p]], preferred_element_type=F32
            )
            total = jnp.where(order_s[side, 2, p] == 1, 0.0, total) + (both[:KH] + both[KH:])
            sums[p] = total
        for at, step in steps.items():
            pl.when(j == at)(step)
        return total

    lax.fori_loop(0, sums.shape[0] // UNROLL, group, jnp.zeros((KH, TILE), F32))

    def collect(j, carry):
        for q in range(4):
            r = j * 4 + q
            store(r, jnp.where(last_s[side, 1, r] == 1, sums[last_s[side, 0, r]], 0.0))
        return carry

    lax.fori_loop(0, UT // 4, collect, 0)


def whole_kernel(user_total, item_total, order_s, last_s, start_ref, user_degree, item_degree, vals_ref, *refs):
    user_out, item_out, vals, turned, split, sums, full_items, full_users, part_users, part_items, raw_users, *refs = refs
    from_core, from_chip, chip_sums, near1, near2, plane1, plane2, user_scale, load_sem, *refs = refs
    send, recv = refs[-2:]
    place = Place()
    xh, y, z = place.xh, place.y, place.z
    sems = Sems(send, recv)
    spread = [Spread(sems, place, full_items.at[h]) for h in range(2)]
    reduce = [
        Reduce(sems, place, part_items.at[h], refs[h * REDUCE_BUFS : (h + 1) * REDUCE_BUFS]) for h in range(2)
    ]
    user = [
        UserSum(sems, place, h, part_users.at[h], full_users.at[h], from_core.at[h], from_chip.at[h], chip_sums.at[h])
        for h in range(2)
    ]
    user_near, item_near = near_sum(sems, place, near1), near_sum(sems, place, near2)
    user_plane, item_plane = plane_sum(sems, place, plane1), plane_sum(sems, place, plane2)
    slots = vals.shape[0]
    portion = slots // LOADS
    loads = [
        pltpu.make_async_copy(
            vals_ref.at[pl.ds(k * portion, portion)], vals.at[pl.ds(k * portion, portion)], load_sem.at[k]
        )
        for k in range(LOADS)
    ]
    for load in loads:
        load.start()
    greet(place.near() + place.plane() + corners(place))

    def turn_tiles(k):
        loads[k].wait()

        def some(j, carry):
            for q in range(8):
                at = k * portion + j * 8 + q
                turned[at] = vals[at].T
            return carry

        lax.fori_loop(0, portion // 8, some, 0)

    def place_of(ref, half, tile):
        return ref.at[half, tile // 32, (tile // 8) % 4, (tile // 2) % 4, tile % 2]

    def to_users(half, steps):
        def store(r, value):
            part_users[half, r] = value

        products(
            order_s, last_s, 0, turned, lambda i: place_of(full_items, half, i)[...], store, split, sums, steps
        )

    def to_items(half, steps):
        def store(r, value):
            place_of(part_items, half, r)[...] = value

        products(order_s, last_s, 1, vals, lambda i: full_users[half, i], store, split, sums, steps)

    item_scale = lax.rsqrt(item_degree[...].astype(F32))
    for h in range(2):
        for t in range(2):
            start = start_ref[h * KH : (h + 1) * KH, t * TILE : (t + 1) * TILE].astype(F32)
            full_items[h, xh, y, z, t] = item_scale[t : t + 1] * start
        spread[h].start()
    user_scale[...] = lax.rsqrt(user_degree[...].astype(F32))
    turn_tiles(0)
    spread[0].turn()
    turn_tiles(1)
    spread[1].turn()
    turn_tiles(2)
    spread[0].last()
    turn_tiles(3)
    spread[0].finish()
    item_factor = None
    for step in range(ITERS):
        first = step == 0

        to_users(0, {3: spread[1].last} if first else {1: spread[1].turn, 5: spread[1].last})
        user[0].start()
        spread[1].finish()
        if not first:
            item_plane.start(item_near.finish())
        to_users(1, {0: user[0].sum, 6: lambda: user[0].combine(0, user_scale, raw_users)})
        user[1].start()
        user[0].combine(1, user_scale, raw_users)
        user[1].sum()
        if not first:
            factor = Factor(item_plane.finish() / item_total)
            factor.columns(0, K)
            item_factor = factor.inverse()
        user[0].hand_on()
        user[1].combine(0, user_scale, raw_users)
        user[0].finish()
        to_items(0, {0: lambda: user[1].combine(1, user_scale, raw_users), 7: user[1].hand_on})
        for part in spread:
            part.drain()
        reduce[0].start()
        if not first:
            for t in range(16):
                raw_users[t] = apply(item_factor, raw_users[t])
        user_plane.start(gram_of([raw_users[t] for t in range(16)]))
        user[1].finish()

        def gram_step():
            user_near.start(user_plane.finish())

        to_items(1, {2: reduce[0].forward, 3: gram_step, 6: reduce[0].turn})
        reduce[1].start()
        factor = Factor(user_near.finish() / user_total)
        factor.columns(0, KH)
        totals = [reduce[0].finish()]
        if first:
            top = factor.inverse()[:KH, :KH]
            raw_top = [apply(top, item_scale[t : t + 1] * totals[0][t]) for t in range(2)]
            for t in range(2):
                full_items[0, xh, y, z, t] = item_scale[t : t + 1] * raw_top[t]
            spread[0].start()
        reduce[1].forward()
        factor.columns(KH, K)
        user_factor = factor.inverse()
        reduce[1].turn()
        if first:
            spread[0].turn()
        else:
            for t in range(16):
                user_out[:, t * TILE : (t + 1) * TILE] = apply(user_factor, raw_users[t])
        totals.append(reduce[1].finish())
        raw_items = []
        for t in range(2):
            raw = item_scale[t : t + 1] * jnp.concatenate([totals[0][t], totals[1][t]], axis=0)
            if first:
                low = apply(user_factor[KH:], raw)
                full_items[1, xh, y, z, t] = item_scale[t : t + 1] * low
                raw_items.append(jnp.concatenate([raw_top[t], low], axis=0))
            else:
                raw_items.append(apply(user_factor, apply(item_factor, raw)))
        if first:
            spread[1].start()
            item_near.start(gram_of(raw_items))
        for part in (*user, *reduce, user_plane, user_near):
            part.drain()
        if first:
            spread[0].last()
            spread[0].finish()
        else:
            item_plane.drain()
            item_near.drain()

    item_near.start(gram_of(raw_items))
    item_plane.start(item_near.finish())
    factor = Factor(item_plane.finish() / item_total)
    factor.columns(0, K)
    last_factor = factor.inverse()
    for t in range(2):
        item_out[:, t * TILE : (t + 1) * TILE] = apply(last_factor, raw_items[t])
    item_near.drain()
    item_plane.drain()


def whole_call(user_total, item_total, order, last, start, user_degree, item_degree, vals):
    slots = vals.shape[0]
    copies = 2 * (SPREAD_COPIES + REDUCE_COPIES + USER_COPIES) + 44
    tiles = pltpu.VMEM((slots, TILE, TILE), jnp.bfloat16)
    full = (2, 2, 4, 4, 2, KH, TILE)
    scratch = [
        tiles,
        tiles,
        pltpu.VMEM((IT, 2 * KH, TILE), jnp.bfloat16),
        pltpu.VMEM((slots, KH, TILE), F32),
        pltpu.VMEM(full, F32),
        pltpu.VMEM((2, UT, KH, TILE), F32),
        pltpu.VMEM((2, UT, KH, TILE), F32),
        pltpu.VMEM(full, F32),
        pltpu.VMEM((16, K, TILE), F32),
        pltpu.VMEM((2, 2, NCH, SIZE, KH, TILE), F32),
        pltpu.VMEM((2, NCH, SIZE, KH, TILE), F32),
        pltpu.VMEM((2, NCH, SIZE, KH, TILE), F32),
        pltpu.VMEM((8, K, K), F32),
        pltpu.VMEM((8, K, K), F32),
        pltpu.VMEM((16, K, K), F32),
        pltpu.VMEM((16, K, K), F32),
        pltpu.VMEM((16, TILE), F32),
        pltpu.SemaphoreType.DMA((LOADS,)),
        *reduce_bufs(),
        *reduce_bufs(),
        pltpu.SemaphoreType.DMA((copies,)),
        pltpu.SemaphoreType.DMA((copies,)),
    ]
    return pl.pallas_call(
        functools.partial(whole_kernel, user_total, item_total),
        out_shape=(
            jax.ShapeDtypeStruct((K, 16 * TILE), F32),
            jax.ShapeDtypeStruct((K, 2 * TILE), F32),
        ),
        in_specs=[SMEM, SMEM, VMEM, VMEM, VMEM, pl.BlockSpec(memory_space=pl.ANY)],
        out_specs=(VMEM, VMEM),
        scratch_shapes=scratch,
        compiler_params=pltpu.CompilerParams(
            collective_id=1, has_side_effects=True, vmem_limit_bytes=VMEM_LIMIT
        ),
        name="cocluster",
    )(order, last, start, user_degree, item_degree, vals)


def slot_order(rows, cols, count):
    slots = rows.shape[0]
    at = jnp.arange(slots, dtype=jnp.int32)
    dead = jnp.where(at < count, 0, UT)
    target = jnp.stack([rows, cols]) + dead
    source = jnp.stack([cols, rows])
    code = (target * IT + source) * slots + at
    rank = jnp.sum((code[:, None, :] < code[:, :, None]).astype(jnp.int32), axis=2)
    ranked = jnp.sum(jnp.where(rank[:, None, :] == at[None, :, None], code[:, None, :], 0), axis=2)
    slot, source, target = ranked % slots, (ranked // slots) % IT, ranked // (slots * IT)
    before = jnp.concatenate([jnp.full((2, 1), -1, jnp.int32), target[:, :-1]], axis=1)
    order = jnp.stack([slot, source, (target != before).astype(jnp.int32)], axis=1)
    line = jnp.arange(UT, dtype=jnp.int32)[None, :, None]
    upto = jnp.sum((target[:, None, :] <= line).astype(jnp.int32), axis=2)
    has = jnp.sum((target[:, None, :] == line).astype(jnp.int32), axis=2)
    last = jnp.stack([jnp.maximum(upto - 1, 0), (has > 0).astype(jnp.int32)], axis=1)
    return order, last


def body(tile_rows, tile_cols, tile_count, tile_vals, user_degree, item_degree, start_items):
    user_total = 16 * TILE * lax.axis_size("users") * lax.axis_size("items")
    item_total = 2 * TILE * lax.axis_size("users") * lax.axis_size("items")
    order, last = slot_order(tile_rows[0, 0], tile_cols[0, 0], tile_count[0, 0])
    degrees = user_degree.reshape(16, TILE), item_degree.reshape(2, TILE)
    return whole_call(user_total, item_total, order, last, start_items, *degrees, tile_vals[0, 0])


def solution(mesh):
    in_specs = (
        P("users", "items", None),
        P("users", "items", None),
        P("users", "items"),
        P("users", "items", None, None, None),
        P(("users", "items")),
        P(("items", "users")),
        P(None, ("items", "users")),
    )
    out_specs = (P(None, ("users", "items")), P(None, ("items", "users")))
    return jax.shard_map(body, mesh=mesh, in_specs=in_specs, out_specs=out_specs, check_vma=False)
```

```python
import functools

import jax
import jax.numpy as jnp
from jax import lax
from jax.experimental import pallas as pl
from jax.experimental.pallas import tpu as pltpu
from jax.sharding import PartitionSpec as P

K = 64
KH = K // 2
H = KH // 2
Q = KH // 4
TILE = 128
UT = 64
IT = 64
ITERS = 2
UNROLL = 64
LOADS = 4
NCH = 2
SIZE = 16 // NCH
MESH = pl.DeviceIdType.MESH
F32 = jnp.float32
HIGHEST = lax.Precision.HIGHEST
VMEM_LIMIT = 63 * 1024 * 1024
VMEM = pl.BlockSpec(memory_space=pltpu.VMEM)
SMEM = pl.BlockSpec(memory_space=pltpu.SMEM)


class Place:
    def __init__(self):
        users = lax.axis_index("users")
        items = lax.axis_index("items")
        self.xh, self.y, self.z = users // 16, (users // 4) % 4, users % 4
        self.xl, self.core = items // 2, items % 2

    def at(self, xh=None, y=None, z=None, xl=None, core=None):
        xh = self.xh if xh is None else xh
        y = self.y if y is None else y
        z = self.z if z is None else z
        xl = self.xl if xl is None else xl
        core = self.core if core is None else core
        return ((xh * 4 + y) * 4 + z, xl * 2 + core)

    def near(self):
        out = []
        for k in range(1, 8):
            j = (self.xh * 4 + self.xl * 2 + self.core + k) % 8
            out.append(self.at(xh=j // 4, xl=(j // 2) % 2, core=j % 2))
        return out

    def plane(self):
        out = []
        for k in range(1, 16):
            j = (self.y * 4 + self.z + k) % 16
            out.append(self.at(y=j // 4, z=j % 4))
        return out


def octet(place, along_y):
    line = place.y if along_y else place.z
    out = []
    for k in range(1, 8):
        j = (place.xh * 4 + line + k) % 8
        out.append((j // 4, j % 4, place.at(xh=j // 4, y=j % 4) if along_y else place.at(xh=j // 4, z=j % 4)))
    return out


def corners(place):
    out = []
    for k in range(1, 4):
        out.append(place.at(xh=1 - place.xh, y=(place.y + k) % 4))
        out.append(place.at(xh=1 - place.xh, z=(place.z + k) % 4))
    return out


def greet(devices):
    barrier = pltpu.get_barrier_semaphore()
    for device in devices:
        pl.semaphore_signal(barrier, inc=1, device_id=device, device_id_type=MESH)
    pl.semaphore_wait(barrier, len(devices))


class Sems:
    def __init__(self, send, recv):
        self.send, self.recv, self.used = send, recv, 0

    def copy(self, src, dst, device):
        k = self.used
        self.used += 1
        return pltpu.make_async_remote_copy(
            src_ref=src,
            dst_ref=dst,
            send_sem=self.send.at[k],
            recv_sem=self.recv.at[k],
            device_id=device,
            device_id_type=MESH,
        )


LOW, HIGH = slice(0, Q), slice(Q, H)


def rows(way, part=None):
    start = way * H + (Q if part is HIGH else 0)
    return pl.ds(start, H if part is None else Q)


class RingGather:
    def __init__(self, sems, slab, me, device):
        plus, minus, far = (me + 1) % 4, (me + 3) % 4, (me + 2) % 4
        to_plus, to_minus = device(plus), device(minus)
        self.own = [
            sems.copy(slab(me, None), slab(me, None), to_plus),
            sems.copy(slab(me, None), slab(me, None), to_minus),
        ]
        self.on = [
            sems.copy(slab(minus, LOW), slab(minus, LOW), to_plus),
            sems.copy(slab(plus, HIGH), slab(plus, HIGH), to_minus),
        ]
        del far

    def start(self):
        for copy in self.own:
            copy.start()

    def forward(self):
        for own, on in zip(self.own, self.on):
            own.wait_recv()
            on.start()

    def finish(self):
        for on in self.on:
            on.wait_recv()

    def drain(self):
        for copy in self.own + self.on:
            copy.wait_send()


class RingReduce:
    def __init__(self, sems, slab, me, device, first, second, sums):
        plus, minus, far = (me + 1) % 4, (me + 3) % 4, (me + 2) % 4
        to_plus, to_minus = device(plus), device(minus)
        self.slab, self.me, self.plus, self.minus = slab, me, plus, minus
        self.first, self.second, self.sums = first, second, sums
        self.far = [
            sems.copy(slab(far, LOW), first.at[0], to_plus),
            sems.copy(slab(far, HIGH), first.at[1], to_minus),
        ]
        self.plain = [
            sems.copy(slab(plus, HIGH), second.at[0, 1], to_plus),
            sems.copy(slab(minus, LOW), second.at[1, 0], to_minus),
        ]
        self.summed = [
            sems.copy(sums.at[0], second.at[0, 0], to_plus),
            sems.copy(sums.at[1], second.at[1, 1], to_minus),
        ]

    def start(self):
        for copy in self.far + self.plain:
            copy.start()

    def forward(self):
        for k, (place, part) in enumerate(((self.plus, LOW), (self.minus, HIGH))):
            self.far[k].wait_recv()
            self.sums[k] = self.slab(place, part)[...] + self.first[k]
            self.summed[k].start()

    def finish(self, out_low, out_high):
        self.plain[1].wait_recv()
        self.summed[0].wait_recv()
        out_low[...] = self.slab(self.me, LOW)[...] + (self.second[0, 0] + self.second[1, 0])
        self.plain[0].wait_recv()
        self.summed[1].wait_recv()
        out_high[...] = self.slab(self.me, HIGH)[...] + (self.second[0, 1] + self.second[1, 1])

    def drain(self):
        for copy in self.far + self.plain + self.summed:
            copy.wait_send()


class GroupSum:
    def __init__(self, sems, buf, index, others):
        self.buf, self.index = buf, index
        self.copies = [sems.copy(buf.at[index], buf.at[index], d) for d in others]

    def start(self, value):
        self.buf[self.index] = value
        for copy in self.copies:
            copy.start()

    def finish(self):
        for copy in self.copies:
            copy.wait_recv()
        total = self.buf[0]
        for k in range(1, self.buf.shape[0]):
            total = total + self.buf[k]
        return total

    def drain(self):
        for copy in self.copies:
            copy.wait_send()


def near_sum(sems, place, buf):
    return GroupSum(sems, buf, place.xh * 4 + place.xl * 2 + place.core, place.near())


def plane_sum(sems, place, buf):
    return GroupSum(sems, buf, place.y * 4 + place.z, place.plane())


class Factor:
    def __init__(self, gram):
        self.row = lax.broadcasted_iota(jnp.int32, (K, 2 * K), 0)
        self.lane = lax.broadcasted_iota(jnp.int32, (K, 2 * K), 1)
        work = jnp.concatenate([gram, jnp.zeros((K, K), F32)], axis=1)
        self.work = work + jnp.where(self.lane == self.row + K, 1.0, 0.0)

    def columns(self, start, stop, step=8):
        work = self.work
        for j in range(start, stop, step):
            cols = [jnp.broadcast_to(work[:, k : k + 1], (K, 2 * K)) for k in range(j, j + step)]
            for s in range(step):
                k = j + s
                factor = jnp.where(self.row > k, cols[s] * (1.0 / cols[s][k : k + 1]), 0.0)
                for m in range(s + 1, step):
                    cols[m] = cols[m] - factor * cols[m][k : k + 1]
                work = work - factor * work[k : k + 1]
        self.work = work

    def inverse(self):
        pivots = jnp.sum(jnp.where(self.lane == self.row, self.work, 0.0), axis=1, keepdims=True)
        return self.work[:, K:] * lax.rsqrt(pivots)


def apply(left, right):
    return jnp.dot(left, right, precision=HIGHEST, preferred_element_type=F32)


def gram_of(tiles):
    total = jnp.zeros((K, K), F32)
    for x in tiles:
        total = total + lax.dot_general(
            x, x, (((1,), (1,)), ((), ())), precision=HIGHEST, preferred_element_type=F32
        )
    return total


class Spread:
    def __init__(self, sems, place, full):
        at_y, at_z = (lambda n: place.at(y=n)), (lambda n: place.at(z=n))
        y, z = place.y, place.z
        self.direct = []
        for way in range(2):
            block = full.at[place.xh, y, z, :, rows(way)]
            self.direct += [sems.copy(block, block, device) for _, _, device in octet(place, way == 0)]
        self.rings = [
            RingGather(sems, lambda n, p: full.at[:, :, n, :, rows(0, p)], z, at_z),
            RingGather(sems, lambda n, p: full.at[:, n, :, :, rows(1, p)], y, at_y),
        ]

    def start(self):
        for copy in self.direct:
            copy.start()

    def turn(self):
        for way, ring in enumerate(self.rings):
            for copy in self.direct[way * 7 : way * 7 + 7]:
                copy.wait_recv()
            ring.start()

    def last(self):
        for ring in self.rings:
            ring.forward()

    def finish(self):
        for ring in self.rings:
            ring.finish()

    def drain(self):
        for copy in self.direct:
            copy.wait_send()
        for ring in self.rings:
            ring.drain()


SPREAD_COPIES = 22


def ring_bufs(lead):
    return [
        pltpu.VMEM((2, *lead, Q, TILE), F32),
        pltpu.VMEM((2, 2, *lead, Q, TILE), F32),
        pltpu.VMEM((2, *lead, Q, TILE), F32),
    ]


def reduce_bufs():
    return (
        ring_bufs((2, 4, 2))
        + ring_bufs((2, 4, 2))
        + [pltpu.VMEM((2, 2, 4, 2, H, TILE), F32), pltpu.VMEM((2, 7, 2, H, TILE), F32)]
    )


REDUCE_BUFS = 8
REDUCE_COPIES = 26


class Reduce:
    def __init__(self, sems, place, partial, bufs):
        at_y, at_z = (lambda n: place.at(y=n)), (lambda n: place.at(z=n))
        y, z = place.y, place.z
        self.ways, self.arrived = bufs[6:8]
        self.place = place
        self.rings = [
            RingReduce(sems, lambda n, p: partial.at[:, :, n, :, rows(0, p)], z, at_z, *bufs[0:3]),
            RingReduce(sems, lambda n, p: partial.at[:, n, :, :, rows(1, p)], y, at_y, *bufs[3:6]),
        ]
        self.direct = [
            [
                sems.copy(self.ways.at[way, xh, line], self.arrived.at[way, k], device)
                for k, (xh, line, device) in enumerate(octet(place, way == 0))
            ]
            for way in range(2)
        ]

    def start(self):
        for ring in self.rings:
            ring.start()

    def forward(self):
        for ring in self.rings:
            ring.forward()

    def turn(self):
        for way, ring in enumerate(self.rings):
            ring.finish(self.ways.at[way, :, :, :, LOW], self.ways.at[way, :, :, :, HIGH])
            for copy in self.direct[way]:
                copy.start()

    def finish(self):
        place = self.place
        sums = []
        for way, line in enumerate((place.y, place.z)):
            total = self.ways[way, place.xh, line]
            for k, copy in enumerate(self.direct[way]):
                copy.wait_recv()
                total = total + self.arrived[way, k]
            sums.append(total)
        return [jnp.concatenate([sums[0][t], sums[1][t]], axis=0) for t in range(2)]

    def drain(self):
        for ring in self.rings:
            ring.drain()
        for copy in self.direct[0] + self.direct[1]:
            copy.wait_send()


class UserSum:
    def __init__(self, sems, place, half, partial, full, from_core, from_chip, sums):
        xl, core = place.xl, place.core
        sibling, partner = place.at(core=1 - core), place.at(xl=1 - xl)
        self.rows = slice(half * KH, (half + 1) * KH)
        self.place, self.partial, self.full = place, partial, full
        self.from_core, self.from_chip, self.sums = from_core, from_chip, sums
        tiles = self.tiles
        chunks = range(NCH)

        def to_core(xq, slot):
            return [sems.copy(partial.at[tiles(xq, 1 - core, j)], from_core.at[slot, j], sibling) for j in chunks]

        self.core_other, self.core_mine = to_core(1 - xl, 0), to_core(xl, 1)
        self.to_chip = [sems.copy(sums.at[j], from_chip.at[j], partner) for j in chunks]
        mine = [full.at[tiles(xl, core, j)] for j in chunks]
        theirs = [full.at[tiles(1 - xl, core, j)] for j in chunks]
        self.done_chip = [sems.copy(m, m, partner) for m in mine]
        self.done_core = [sems.copy(m, m, sibling) for m in mine]
        self.passed = [sems.copy(t, t, sibling) for t in theirs]

    def tiles(self, xq, cq, j):
        return pl.ds((xq * 2 + cq) * 16 + j * SIZE, SIZE)

    def start(self):
        for copy in self.core_other + self.core_mine:
            copy.start()

    def sum(self):
        place = self.place
        for j in range(NCH):
            self.core_other[j].wait_recv()
            self.sums[j] = self.partial[self.tiles(1 - place.xl, place.core, j)] + self.from_core[0, j]
            self.to_chip[j].start()

    def combine(self, j, scale_ref, raw_ref):
        place = self.place
        self.core_mine[j].wait_recv()
        self.to_chip[j].wait_recv()
        for t in range(SIZE):
            row = j * SIZE + t
            tile = (place.xl * 2 + place.core) * 16 + row
            scale = scale_ref[row : row + 1]
            raw = scale * (self.partial[tile] + (self.from_core[1, j, t] + self.from_chip[j, t]))
            self.full[tile] = scale * raw
            raw_ref[row, self.rows] = raw
        self.done_chip[j].start()
        self.done_core[j].start()

    def hand_on(self):
        for j in range(NCH):
            self.done_chip[j].wait_recv()
            self.passed[j].start()

    def finish(self):
        for j in range(NCH):
            self.done_core[j].wait_recv()
            self.passed[j].wait_recv()

    def drain(self):
        for copy in self.core_other + self.core_mine + self.to_chip + self.done_chip + self.done_core + self.passed:
            copy.wait_send()


USER_COPIES = 6 * NCH


def products(order_s, last_s, side, tiles, load, store, split, sums, steps):
    def prepare(j, carry):
        for q in range(4):
            x = load(j * 4 + q)
            high = x.astype(jnp.bfloat16)
            split[j * 4 + q, :KH] = high
            split[j * 4 + q, KH:] = (x - high.astype(F32)).astype(jnp.bfloat16)
        return carry

    lax.fori_loop(0, IT // 4, prepare, 0)
    split[IT] = jnp.zeros((2 * KH, TILE), jnp.bfloat16)

    def group(j, total):
        for q in range(UNROLL // 2):
            p = j * UNROLL + 2 * q
            panel = jnp.concatenate([split[order_s[side, 1, p]], split[order_s[side, 1, p + 1]]], axis=1)
            pair = jnp.concatenate([tiles[order_s[side, 0, p]], tiles[order_s[side, 0, p + 1]]], axis=0)
            both = jnp.dot(panel, pair, preferred_element_type=F32)
            total = jnp.where(order_s[side, 2, p] == 1, 0.0, total) + (both[:KH] + both[KH:])
            sums[j * (UNROLL // 2) + q] = total
        for at, step in steps.items():
            pl.when(j == at)(step)
        return total

    lax.fori_loop(0, 2 * sums.shape[0] // UNROLL, group, jnp.zeros((KH, TILE), F32))

    def collect(j, carry):
        for q in range(4):
            r = j * 4 + q
            store(r, jnp.where(last_s[side, 1, r] == 1, sums[last_s[side, 0, r]], 0.0))
        return carry

    lax.fori_loop(0, UT // 4, collect, 0)


def whole_kernel(user_total, item_total, order_s, last_s, start_ref, user_degree, item_degree, vals_ref, *refs):
    user_out, item_out, vals, turned, split, sums, full_items, full_users, part_users, part_items, raw_users, *refs = refs
    from_core, from_chip, chip_sums, near1, near2, plane1, plane2, user_scale, load_sem, *refs = refs
    send, recv = refs[-2:]
    place = Place()
    xh, y, z = place.xh, place.y, place.z
    sems = Sems(send, recv)
    spread = [Spread(sems, place, full_items.at[h]) for h in range(2)]
    reduce = [
        Reduce(sems, place, part_items.at[h], refs[h * REDUCE_BUFS : (h + 1) * REDUCE_BUFS]) for h in range(2)
    ]
    user = [
        UserSum(sems, place, h, part_users.at[h], full_users.at[h], from_core.at[h], from_chip.at[h], chip_sums.at[h])
        for h in range(2)
    ]
    user_near, item_near = near_sum(sems, place, near1), near_sum(sems, place, near2)
    user_plane, item_plane = plane_sum(sems, place, plane1), plane_sum(sems, place, plane2)
    slots = vals.shape[0]
    portion = slots // LOADS
    loads = [
        pltpu.make_async_copy(
            vals_ref.at[pl.ds(k * portion, portion)], vals.at[pl.ds(k * portion, portion)], load_sem.at[k]
        )
        for k in range(LOADS)
    ]
    for load in loads:
        load.start()
    greet(place.near() + place.plane() + corners(place))

    def turn_tiles(k):
        loads[k].wait()

        def some(j, carry):
            for q in range(8):
                at = k * portion + j * 8 + q
                turned[at] = vals[at].T
            return carry

        lax.fori_loop(0, portion // 8, some, 0)

    def place_of(ref, half, tile):
        return ref.at[half, tile // 32, (tile // 8) % 4, (tile // 2) % 4, tile % 2]

    def to_users(half, steps):
        def store(r, value):
            part_users[half, r] = value

        products(
            order_s, last_s, 0, turned, lambda i: place_of(full_items, half, i)[...], store, split, sums, steps
        )

    def to_items(half, steps):
        def store(r, value):
            place_of(part_items, half, r)[...] = value

        products(order_s, last_s, 1, vals, lambda i: full_users[half, i], store, split, sums, steps)

    item_scale = lax.rsqrt(item_degree[...].astype(F32))
    for h in range(2):
        for t in range(2):
            start = start_ref[h * KH : (h + 1) * KH, t * TILE : (t + 1) * TILE].astype(F32)
            full_items[h, xh, y, z, t] = item_scale[t : t + 1] * start
        spread[h].start()
    user_scale[...] = lax.rsqrt(user_degree[...].astype(F32))
    turn_tiles(0)
    spread[0].turn()
    turn_tiles(1)
    spread[1].turn()
    turn_tiles(2)
    spread[0].last()
    turn_tiles(3)
    spread[0].finish()
    item_factor = None
    for step in range(ITERS):
        first = step == 0

        to_users(0, {3: spread[1].last} if first else {1: spread[1].turn, 5: spread[1].last})
        user[0].start()
        spread[1].finish()
        if not first:
            item_plane.start(item_near.finish())
        to_users(1, {0: user[0].sum, 6: lambda: user[0].combine(0, user_scale, raw_users)})
        user[1].start()
        user[0].combine(1, user_scale, raw_users)
        user[1].sum()
        if not first:
            factor = Factor(item_plane.finish() / item_total)
            factor.columns(0, K)
            item_factor = factor.inverse()
        user[0].hand_on()
        user[1].combine(0, user_scale, raw_users)
        user[0].finish()

        def users_gram():
            if not first:
                for t in range(16):
                    raw_users[t] = apply(item_factor, raw_users[t])
            user_plane.start(gram_of([raw_users[t] for t in range(16)]))

        to_items(
            0, {0: lambda: user[1].combine(1, user_scale, raw_users), 4: users_gram, 7: user[1].hand_on}
        )
        for part in spread:
            part.drain()
        reduce[0].start()
        user[1].finish()

        def gram_step():
            user_near.start(user_plane.finish())

        to_items(1, {0: gram_step, 2: reduce[0].forward, 6: reduce[0].turn})
        reduce[1].start()
        factor = Factor(user_near.finish() / user_total)
        factor.columns(0, KH)
        totals = [reduce[0].finish()]
        if first:
            top = factor.inverse()[:KH, :KH]
            raw_top = [apply(top, item_scale[t : t + 1] * totals[0][t]) for t in range(2)]
            for t in range(2):
                full_items[0, xh, y, z, t] = item_scale[t : t + 1] * raw_top[t]
            spread[0].start()
        reduce[1].forward()
        factor.columns(KH, K)
        user_factor = factor.inverse()
        reduce[1].turn()
        if first:
            spread[0].turn()
        else:
            for t in range(16):
                user_out[:, t * TILE : (t + 1) * TILE] = apply(user_factor, raw_users[t])
        totals.append(reduce[1].finish())
        raw_items = []
        for t in range(2):
            raw = item_scale[t : t + 1] * jnp.concatenate([totals[0][t], totals[1][t]], axis=0)
            if first:
                low = apply(user_factor[KH:], raw)
                full_items[1, xh, y, z, t] = item_scale[t : t + 1] * low
                raw_items.append(jnp.concatenate([raw_top[t], low], axis=0))
            else:
                raw_items.append(apply(user_factor, apply(item_factor, raw)))
        if first:
            spread[1].start()
            item_near.start(gram_of(raw_items))
        for part in (*user, *reduce, user_plane, user_near):
            part.drain()
        if first:
            spread[0].last()
            spread[0].finish()
        else:
            item_plane.drain()
            item_near.drain()

    item_near.start(gram_of(raw_items))
    item_plane.start(item_near.finish())
    factor = Factor(item_plane.finish() / item_total)
    factor.columns(0, K)
    last_factor = factor.inverse()
    for t in range(2):
        item_out[:, t * TILE : (t + 1) * TILE] = apply(last_factor, raw_items[t])
    item_near.drain()
    item_plane.drain()


def whole_call(user_total, item_total, order, last, start, user_degree, item_degree, vals):
    slots = vals.shape[0]
    copies = 2 * (SPREAD_COPIES + REDUCE_COPIES + USER_COPIES) + 44
    tiles = pltpu.VMEM((slots, TILE, TILE), jnp.bfloat16)
    full = (2, 2, 4, 4, 2, KH, TILE)
    scratch = [
        tiles,
        tiles,
        pltpu.VMEM((IT + 1, 2 * KH, TILE), jnp.bfloat16),
        pltpu.VMEM(((slots + UT) // 2, KH, TILE), F32),
        pltpu.VMEM(full, F32),
        pltpu.VMEM((2, UT, KH, TILE), F32),
        pltpu.VMEM((2, UT, KH, TILE), F32),
        pltpu.VMEM(full, F32),
        pltpu.VMEM((16, K, TILE), F32),
        pltpu.VMEM((2, 2, NCH, SIZE, KH, TILE), F32),
        pltpu.VMEM((2, NCH, SIZE, KH, TILE), F32),
        pltpu.VMEM((2, NCH, SIZE, KH, TILE), F32),
        pltpu.VMEM((8, K, K), F32),
        pltpu.VMEM((8, K, K), F32),
        pltpu.VMEM((16, K, K), F32),
        pltpu.VMEM((16, K, K), F32),
        pltpu.VMEM((16, TILE), F32),
        pltpu.SemaphoreType.DMA((LOADS,)),
        *reduce_bufs(),
        *reduce_bufs(),
        pltpu.SemaphoreType.DMA((copies,)),
        pltpu.SemaphoreType.DMA((copies,)),
    ]
    return pl.pallas_call(
        functools.partial(whole_kernel, user_total, item_total),
        out_shape=(
            jax.ShapeDtypeStruct((K, 16 * TILE), F32),
            jax.ShapeDtypeStruct((K, 2 * TILE), F32),
        ),
        in_specs=[SMEM, SMEM, VMEM, VMEM, VMEM, pl.BlockSpec(memory_space=pl.ANY)],
        out_specs=(VMEM, VMEM),
        scratch_shapes=scratch,
        compiler_params=pltpu.CompilerParams(
            collective_id=1, has_side_effects=True, vmem_limit_bytes=VMEM_LIMIT
        ),
        name="cocluster",
    )(order, last, start, user_degree, item_degree, vals)


def slot_order(rows, cols, count):
    slots = rows.shape[0]
    at = jnp.arange(slots, dtype=jnp.int32)
    dead = jnp.where(at < count, 0, UT)
    target = jnp.stack([rows, cols]) + dead
    source = jnp.stack([cols, rows])
    code = (target * IT + source) * slots + at
    rank = jnp.sum((code[:, None, :] < code[:, :, None]).astype(jnp.int32), axis=2)
    line = jnp.arange(UT, dtype=jnp.int32)
    has = jnp.sum((target[:, None, :] == line[None, :, None]).astype(jnp.int32), axis=2)
    odd = has % 2
    moved = jnp.sum(jnp.where(line[None, :, None] < target[:, None, :], odd[:, :, None], 0), axis=1)
    place = jnp.arange(slots + UT, dtype=jnp.int32)[None, :, None]
    ranked = jnp.sum(jnp.where((rank + moved)[:, None, :] == place, code[:, None, :] + 1, 0), axis=2) - 1
    none = ranked < 0
    slot = jnp.where(none, 0, ranked % slots)
    source = jnp.where(none, IT, (ranked // slots) % IT)
    target = ranked // (slots * IT)
    before = jnp.concatenate([jnp.full((2, 2), -1, jnp.int32), target[:, :-2]], axis=1)
    order = jnp.stack([slot, source, (target != before).astype(jnp.int32)], axis=1)
    upto = jnp.sum(jnp.where(line[None, None, :] <= line[None, :, None], (has + odd)[:, None, :], 0), axis=2)
    last = jnp.stack([jnp.maximum(upto // 2 - 1, 0), (has > 0).astype(jnp.int32)], axis=1)
    return order, last


def body(tile_rows, tile_cols, tile_count, tile_vals, user_degree, item_degree, start_items):
    user_total = 16 * TILE * lax.axis_size("users") * lax.axis_size("items")
    item_total = 2 * TILE * lax.axis_size("users") * lax.axis_size("items")
    order, last = slot_order(tile_rows[0, 0], tile_cols[0, 0], tile_count[0, 0])
    degrees = user_degree.reshape(16, TILE), item_degree.reshape(2, TILE)
    return whole_call(user_total, item_total, order, last, start_items, *degrees, tile_vals[0, 0])


def solution(mesh):
    in_specs = (
        P("users", "items", None),
        P("users", "items", None),
        P("users", "items"),
        P("users", "items", None, None, None),
        P(("users", "items")),
        P(("items", "users")),
        P(None, ("items", "users")),
    )
    out_specs = (P(None, ("users", "items")), P(None, ("items", "users")))
    return jax.shard_map(body, mesh=mesh, in_specs=in_specs, out_specs=out_specs, check_vma=False)
```

```python
import functools

import jax
import jax.numpy as jnp
from jax import lax
from jax.experimental import pallas as pl
from jax.experimental.pallas import tpu as pltpu
from jax.sharding import PartitionSpec as P

K = 64
KH = K // 2
H = KH // 2
Q = KH // 4
TILE = 128
UT = 64
IT = 64
ITERS = 2
UNROLL = 72
LOADS = 4
NCH = 2
SIZE = 16 // NCH
MESH = pl.DeviceIdType.MESH
F32 = jnp.float32
HIGHEST = lax.Precision.HIGHEST
VMEM_LIMIT = 63 * 1024 * 1024
VMEM = pl.BlockSpec(memory_space=pltpu.VMEM)
SMEM = pl.BlockSpec(memory_space=pltpu.SMEM)


class Place:
    def __init__(self):
        users = lax.axis_index("users")
        items = lax.axis_index("items")
        self.xh, self.y, self.z = users // 16, (users // 4) % 4, users % 4
        self.xl, self.core = items // 2, items % 2

    def at(self, xh=None, y=None, z=None, xl=None, core=None):
        xh = self.xh if xh is None else xh
        y = self.y if y is None else y
        z = self.z if z is None else z
        xl = self.xl if xl is None else xl
        core = self.core if core is None else core
        return ((xh * 4 + y) * 4 + z, xl * 2 + core)

    def near(self):
        out = []
        for k in range(1, 8):
            j = (self.xh * 4 + self.xl * 2 + self.core + k) % 8
            out.append(self.at(xh=j // 4, xl=(j // 2) % 2, core=j % 2))
        return out

    def plane(self):
        out = []
        for k in range(1, 16):
            j = (self.y * 4 + self.z + k) % 16
            out.append(self.at(y=j // 4, z=j % 4))
        return out


def octet(place, along_y):
    line = place.y if along_y else place.z
    out = []
    for k in range(1, 8):
        j = (place.xh * 4 + line + k) % 8
        out.append((j // 4, j % 4, place.at(xh=j // 4, y=j % 4) if along_y else place.at(xh=j // 4, z=j % 4)))
    return out


def corners(place):
    out = []
    for k in range(1, 4):
        out.append(place.at(xh=1 - place.xh, y=(place.y + k) % 4))
        out.append(place.at(xh=1 - place.xh, z=(place.z + k) % 4))
    return out


def greet(devices):
    barrier = pltpu.get_barrier_semaphore()
    for device in devices:
        pl.semaphore_signal(barrier, inc=1, device_id=device, device_id_type=MESH)
    pl.semaphore_wait(barrier, len(devices))


class Sems:
    def __init__(self, send, recv):
        self.send, self.recv, self.used = send, recv, 0

    def copy(self, src, dst, device):
        k = self.used
        self.used += 1
        return pltpu.make_async_remote_copy(
            src_ref=src,
            dst_ref=dst,
            send_sem=self.send.at[k],
            recv_sem=self.recv.at[k],
            device_id=device,
            device_id_type=MESH,
        )


LOW, HIGH = slice(0, Q), slice(Q, H)


def rows(way, part=None):
    start = way * H + (Q if part is HIGH else 0)
    return pl.ds(start, H if part is None else Q)


class RingGather:
    def __init__(self, sems, slab, me, device):
        plus, minus, far = (me + 1) % 4, (me + 3) % 4, (me + 2) % 4
        to_plus, to_minus = device(plus), device(minus)
        self.own = [
            sems.copy(slab(me, None), slab(me, None), to_plus),
            sems.copy(slab(me, None), slab(me, None), to_minus),
        ]
        self.on = [
            sems.copy(slab(minus, LOW), slab(minus, LOW), to_plus),
            sems.copy(slab(plus, HIGH), slab(plus, HIGH), to_minus),
        ]
        del far

    def start(self):
        for copy in self.own:
            copy.start()

    def forward(self):
        for own, on in zip(self.own, self.on):
            own.wait_recv()
            on.start()

    def finish(self):
        for on in self.on:
            on.wait_recv()

    def drain(self):
        for copy in self.own + self.on:
            copy.wait_send()


class RingReduce:
    def __init__(self, sems, slab, me, device, first, second, sums):
        plus, minus, far = (me + 1) % 4, (me + 3) % 4, (me + 2) % 4
        to_plus, to_minus = device(plus), device(minus)
        self.slab, self.me, self.plus, self.minus = slab, me, plus, minus
        self.first, self.second, self.sums = first, second, sums
        self.far = [
            sems.copy(slab(far, LOW), first.at[0], to_plus),
            sems.copy(slab(far, HIGH), first.at[1], to_minus),
        ]
        self.plain = [
            sems.copy(slab(plus, HIGH), second.at[0, 1], to_plus),
            sems.copy(slab(minus, LOW), second.at[1, 0], to_minus),
        ]
        self.summed = [
            sems.copy(sums.at[0], second.at[0, 0], to_plus),
            sems.copy(sums.at[1], second.at[1, 1], to_minus),
        ]

    def start(self):
        for copy in self.far + self.plain:
            copy.start()

    def forward(self):
        for k, (place, part) in enumerate(((self.plus, LOW), (self.minus, HIGH))):
            self.far[k].wait_recv()
            self.sums[k] = self.slab(place, part)[...] + self.first[k]
            self.summed[k].start()

    def finish(self, out_low, out_high):
        self.plain[1].wait_recv()
        self.summed[0].wait_recv()
        out_low[...] = self.slab(self.me, LOW)[...] + (self.second[0, 0] + self.second[1, 0])
        self.plain[0].wait_recv()
        self.summed[1].wait_recv()
        out_high[...] = self.slab(self.me, HIGH)[...] + (self.second[0, 1] + self.second[1, 1])

    def drain(self):
        for copy in self.far + self.plain + self.summed:
            copy.wait_send()


class GroupSum:
    def __init__(self, sems, buf, index, others):
        self.buf, self.index = buf, index
        self.copies = [sems.copy(buf.at[index], buf.at[index], d) for d in others]

    def start(self, value):
        self.buf[self.index] = value
        for copy in self.copies:
            copy.start()

    def finish(self):
        for copy in self.copies:
            copy.wait_recv()
        total = self.buf[0]
        for k in range(1, self.buf.shape[0]):
            total = total + self.buf[k]
        return total

    def drain(self):
        for copy in self.copies:
            copy.wait_send()


def near_sum(sems, place, buf):
    return GroupSum(sems, buf, place.xh * 4 + place.xl * 2 + place.core, place.near())


def plane_sum(sems, place, buf):
    return GroupSum(sems, buf, place.y * 4 + place.z, place.plane())


class Factor:
    def __init__(self, gram):
        self.row = lax.broadcasted_iota(jnp.int32, (K, 2 * K), 0)
        self.lane = lax.broadcasted_iota(jnp.int32, (K, 2 * K), 1)
        work = jnp.concatenate([gram, jnp.zeros((K, K), F32)], axis=1)
        self.work = work + jnp.where(self.lane == self.row + K, 1.0, 0.0)

    def columns(self, start, stop, step=8):
        work = self.work
        for j in range(start, stop, step):
            cols = [jnp.broadcast_to(work[:, k : k + 1], (K, 2 * K)) for k in range(j, j + step)]
            for s in range(step):
                k = j + s
                factor = jnp.where(self.row > k, cols[s] * (1.0 / cols[s][k : k + 1]), 0.0)
                for m in range(s + 1, step):
                    cols[m] = cols[m] - factor * cols[m][k : k + 1]
                work = work - factor * work[k : k + 1]
        self.work = work

    def inverse(self):
        pivots = jnp.sum(jnp.where(self.lane == self.row, self.work, 0.0), axis=1, keepdims=True)
        return self.work[:, K:] * lax.rsqrt(pivots)


def apply(left, right):
    return jnp.dot(left, right, precision=HIGHEST, preferred_element_type=F32)


def gram_of(tiles):
    total = jnp.zeros((K, K), F32)
    for x in tiles:
        total = total + lax.dot_general(
            x, x, (((1,), (1,)), ((), ())), precision=HIGHEST, preferred_element_type=F32
        )
    return total


class Spread:
    def __init__(self, sems, place, full):
        at_y, at_z = (lambda n: place.at(y=n)), (lambda n: place.at(z=n))
        y, z = place.y, place.z
        self.direct = []
        for way in range(2):
            block = full.at[place.xh, y, z, :, rows(way)]
            self.direct += [sems.copy(block, block, device) for _, _, device in octet(place, way == 0)]
        self.rings = [
            RingGather(sems, lambda n, p: full.at[:, :, n, :, rows(0, p)], z, at_z),
            RingGather(sems, lambda n, p: full.at[:, n, :, :, rows(1, p)], y, at_y),
        ]

    def start(self):
        for copy in self.direct:
            copy.start()

    def turn(self):
        for way, ring in enumerate(self.rings):
            for copy in self.direct[way * 7 : way * 7 + 7]:
                copy.wait_recv()
            ring.start()

    def last(self):
        for ring in self.rings:
            ring.forward()

    def finish(self):
        for ring in self.rings:
            ring.finish()

    def drain(self):
        for copy in self.direct:
            copy.wait_send()
        for ring in self.rings:
            ring.drain()


SPREAD_COPIES = 22


def ring_bufs(lead):
    return [
        pltpu.VMEM((2, *lead, Q, TILE), F32),
        pltpu.VMEM((2, 2, *lead, Q, TILE), F32),
        pltpu.VMEM((2, *lead, Q, TILE), F32),
    ]


def reduce_bufs():
    return (
        ring_bufs((2, 4, 2))
        + ring_bufs((2, 4, 2))
        + [pltpu.VMEM((2, 2, 4, 2, H, TILE), F32), pltpu.VMEM((2, 7, 2, H, TILE), F32)]
    )


REDUCE_BUFS = 8
REDUCE_COPIES = 26


class Reduce:
    def __init__(self, sems, place, partial, bufs):
        at_y, at_z = (lambda n: place.at(y=n)), (lambda n: place.at(z=n))
        y, z = place.y, place.z
        self.ways, self.arrived = bufs[6:8]
        self.place = place
        self.rings = [
            RingReduce(sems, lambda n, p: partial.at[:, :, n, :, rows(0, p)], z, at_z, *bufs[0:3]),
            RingReduce(sems, lambda n, p: partial.at[:, n, :, :, rows(1, p)], y, at_y, *bufs[3:6]),
        ]
        self.direct = [
            [
                sems.copy(self.ways.at[way, xh, line], self.arrived.at[way, k], device)
                for k, (xh, line, device) in enumerate(octet(place, way == 0))
            ]
            for way in range(2)
        ]

    def start(self):
        for ring in self.rings:
            ring.start()

    def forward(self):
        for ring in self.rings:
            ring.forward()

    def turn(self):
        for way, ring in enumerate(self.rings):
            ring.finish(self.ways.at[way, :, :, :, LOW], self.ways.at[way, :, :, :, HIGH])
            for copy in self.direct[way]:
                copy.start()

    def finish(self):
        place = self.place
        sums = []
        for way, line in enumerate((place.y, place.z)):
            total = self.ways[way, place.xh, line]
            for k, copy in enumerate(self.direct[way]):
                copy.wait_recv()
                total = total + self.arrived[way, k]
            sums.append(total)
        return [jnp.concatenate([sums[0][t], sums[1][t]], axis=0) for t in range(2)]

    def drain(self):
        for ring in self.rings:
            ring.drain()
        for copy in self.direct[0] + self.direct[1]:
            copy.wait_send()


class UserSum:
    def __init__(self, sems, place, half, partial, full, from_core, from_chip, sums):
        xl, core = place.xl, place.core
        sibling, partner = place.at(core=1 - core), place.at(xl=1 - xl)
        self.rows = slice(half * KH, (half + 1) * KH)
        self.place, self.partial, self.full = place, partial, full
        self.from_core, self.from_chip, self.sums = from_core, from_chip, sums
        tiles = self.tiles
        chunks = range(NCH)

        def to_core(xq, slot):
            return [sems.copy(partial.at[tiles(xq, 1 - core, j)], from_core.at[slot, j], sibling) for j in chunks]

        self.core_other, self.core_mine = to_core(1 - xl, 0), to_core(xl, 1)
        self.to_chip = [sems.copy(sums.at[j], from_chip.at[j], partner) for j in chunks]
        mine = [full.at[tiles(xl, core, j)] for j in chunks]
        theirs = [full.at[tiles(1 - xl, core, j)] for j in chunks]
        self.done_chip = [sems.copy(m, m, partner) for m in mine]
        self.done_core = [sems.copy(m, m, sibling) for m in mine]
        self.passed = [sems.copy(t, t, sibling) for t in theirs]

    def tiles(self, xq, cq, j):
        return pl.ds((xq * 2 + cq) * 16 + j * SIZE, SIZE)

    def start(self):
        for copy in self.core_other + self.core_mine:
            copy.start()

    def sum(self):
        place = self.place
        for j in range(NCH):
            self.core_other[j].wait_recv()
            self.sums[j] = self.partial[self.tiles(1 - place.xl, place.core, j)] + self.from_core[0, j]
            self.to_chip[j].start()

    def combine(self, j, scale_ref, raw_ref):
        place = self.place
        self.core_mine[j].wait_recv()
        self.to_chip[j].wait_recv()
        for t in range(SIZE):
            row = j * SIZE + t
            tile = (place.xl * 2 + place.core) * 16 + row
            scale = scale_ref[row : row + 1]
            raw = scale * (self.partial[tile] + (self.from_core[1, j, t] + self.from_chip[j, t]))
            self.full[tile] = scale * raw
            raw_ref[row, self.rows] = raw
        self.done_chip[j].start()
        self.done_core[j].start()

    def hand_on(self):
        for j in range(NCH):
            self.done_chip[j].wait_recv()
            self.passed[j].start()

    def finish(self):
        for j in range(NCH):
            self.done_core[j].wait_recv()
            self.passed[j].wait_recv()

    def drain(self):
        for copy in self.core_other + self.core_mine + self.to_chip + self.done_chip + self.done_core + self.passed:
            copy.wait_send()


USER_COPIES = 6 * NCH


def products(order_s, last_s, side, tiles, load, store, split, sums, steps):
    def prepare(j, carry):
        for q in range(4):
            x = load(j * 4 + q)
            high = x.astype(jnp.bfloat16)
            split[j * 4 + q, :KH] = high
            split[j * 4 + q, KH:] = (x - high.astype(F32)).astype(jnp.bfloat16)
        return carry

    lax.fori_loop(0, IT // 4, prepare, 0)
    split[IT] = jnp.zeros((2 * KH, TILE), jnp.bfloat16)

    def group(j, total):
        for q in range(UNROLL // 2):
            p = j * UNROLL + 2 * q
            panel = jnp.concatenate([split[order_s[side, 1, p]], split[order_s[side, 1, p + 1]]], axis=1)
            pair = jnp.concatenate([tiles[order_s[side, 0, p]], tiles[order_s[side, 0, p + 1]]], axis=0)
            both = jnp.dot(panel, pair, preferred_element_type=F32)
            total = jnp.where(order_s[side, 2, p] == 1, 0.0, total) + (both[:KH] + both[KH:])
            sums[j * (UNROLL // 2) + q] = total
        for at, step in steps.items():
            pl.when(j == at)(step)
        return total

    lax.fori_loop(0, 2 * sums.shape[0] // UNROLL, group, jnp.zeros((KH, TILE), F32))

    def collect(j, carry):
        for q in range(4):
            r = j * 4 + q
            store(r, jnp.where(last_s[side, 1, r] == 1, sums[last_s[side, 0, r]], 0.0))
        return carry

    lax.fori_loop(0, UT // 4, collect, 0)


def whole_kernel(user_total, item_total, order_s, last_s, start_ref, user_degree, item_degree, vals_ref, *refs):
    user_out, item_out, vals, turned, split, sums, full_items, full_users, part_users, part_items, raw_users, *refs = refs
    from_core, from_chip, chip_sums, near1, near2, plane1, plane2, user_scale, load_sem, *refs = refs
    send, recv = refs[-2:]
    place = Place()
    xh, y, z = place.xh, place.y, place.z
    sems = Sems(send, recv)
    spread = [Spread(sems, place, full_items.at[h]) for h in range(2)]
    reduce = [
        Reduce(sems, place, part_items.at[h], refs[h * REDUCE_BUFS : (h + 1) * REDUCE_BUFS]) for h in range(2)
    ]
    user = [
        UserSum(sems, place, h, part_users.at[h], full_users.at[h], from_core.at[h], from_chip.at[h], chip_sums.at[h])
        for h in range(2)
    ]
    user_near, item_near = near_sum(sems, place, near1), near_sum(sems, place, near2)
    user_plane, item_plane = plane_sum(sems, place, plane1), plane_sum(sems, place, plane2)
    slots = vals.shape[0]
    portion = slots // LOADS
    loads = [
        pltpu.make_async_copy(
            vals_ref.at[pl.ds(k * portion, portion)], vals.at[pl.ds(k * portion, portion)], load_sem.at[k]
        )
        for k in range(LOADS)
    ]
    for load in loads:
        load.start()
    greet(place.near() + place.plane() + corners(place))

    def turn_tiles(k):
        loads[k].wait()

        def some(j, carry):
            for q in range(8):
                at = k * portion + j * 8 + q
                turned[at] = vals[at].T
            return carry

        lax.fori_loop(0, portion // 8, some, 0)

    def place_of(ref, half, tile):
        return ref.at[half, tile // 32, (tile // 8) % 4, (tile // 2) % 4, tile % 2]

    def to_users(half, steps):
        def store(r, value):
            part_users[half, r] = value

        products(
            order_s, last_s, 0, turned, lambda i: place_of(full_items, half, i)[...], store, split, sums, steps
        )

    def to_items(half, steps):
        def store(r, value):
            place_of(part_items, half, r)[...] = value

        products(order_s, last_s, 1, vals, lambda i: full_users[half, i], store, split, sums, steps)

    item_scale = lax.rsqrt(item_degree[...].astype(F32))
    for h in range(2):
        for t in range(2):
            start = start_ref[h * KH : (h + 1) * KH, t * TILE : (t + 1) * TILE].astype(F32)
            full_items[h, xh, y, z, t] = item_scale[t : t + 1] * start
        spread[h].start()
    user_scale[...] = lax.rsqrt(user_degree[...].astype(F32))
    turn_tiles(0)
    spread[0].turn()
    turn_tiles(1)
    spread[1].turn()
    turn_tiles(2)
    spread[0].last()
    turn_tiles(3)
    spread[0].finish()
    item_factor = None
    for step in range(ITERS):
        first = step == 0

        to_users(0, {3: spread[1].last} if first else {1: spread[1].turn, 5: spread[1].last})
        user[0].start()
        spread[1].finish()
        if not first:
            item_plane.start(item_near.finish())
        to_users(1, {0: user[0].sum, 6: lambda: user[0].combine(0, user_scale, raw_users)})
        user[1].start()
        user[0].combine(1, user_scale, raw_users)
        user[1].sum()
        if not first:
            factor = Factor(item_plane.finish() / item_total)
            factor.columns(0, K)
            item_factor = factor.inverse()
        user[0].hand_on()
        user[1].combine(0, user_scale, raw_users)
        user[0].finish()

        def users_gram():
            if not first:
                for t in range(16):
                    raw_users[t] = apply(item_factor, raw_users[t])
            user_plane.start(gram_of([raw_users[t] for t in range(16)]))

        to_items(
            0, {0: lambda: user[1].combine(1, user_scale, raw_users), 4: users_gram, 7: user[1].hand_on}
        )
        for part in spread:
            part.drain()
        reduce[0].start()
        user[1].finish()

        def gram_step():
            user_near.start(user_plane.finish())

        to_items(1, {0: gram_step, 2: reduce[0].forward, 6: reduce[0].turn})
        reduce[1].start()
        factor = Factor(user_near.finish() / user_total)
        factor.columns(0, KH)
        totals = [reduce[0].finish()]
        if first:
            top = factor.inverse()[:KH, :KH]
            raw_top = [apply(top, item_scale[t : t + 1] * totals[0][t]) for t in range(2)]
            for t in range(2):
                full_items[0, xh, y, z, t] = item_scale[t : t + 1] * raw_top[t]
            spread[0].start()
        reduce[1].forward()
        factor.columns(KH, K)
        user_factor = factor.inverse()
        reduce[1].turn()
        if first:
            spread[0].turn()
        else:
            for t in range(16):
                user_out[:, t * TILE : (t + 1) * TILE] = apply(user_factor, raw_users[t])
        totals.append(reduce[1].finish())
        raw_items = []
        for t in range(2):
            raw = item_scale[t : t + 1] * jnp.concatenate([totals[0][t], totals[1][t]], axis=0)
            if first:
                low = apply(user_factor[KH:], raw)
                full_items[1, xh, y, z, t] = item_scale[t : t + 1] * low
                raw_items.append(jnp.concatenate([raw_top[t], low], axis=0))
            else:
                raw_items.append(apply(user_factor, apply(item_factor, raw)))
        if first:
            spread[1].start()
            item_near.start(gram_of(raw_items))
        for part in (*user, *reduce, user_plane, user_near):
            part.drain()
        if first:
            spread[0].last()
            spread[0].finish()
        else:
            item_plane.drain()
            item_near.drain()

    item_near.start(gram_of(raw_items))
    item_plane.start(item_near.finish())
    factor = Factor(item_plane.finish() / item_total)
    factor.columns(0, K)
    last_factor = factor.inverse()
    for t in range(2):
        item_out[:, t * TILE : (t + 1) * TILE] = apply(last_factor, raw_items[t])
    item_near.drain()
    item_plane.drain()


def whole_call(user_total, item_total, order, last, start, user_degree, item_degree, vals):
    slots = vals.shape[0]
    copies = 2 * (SPREAD_COPIES + REDUCE_COPIES + USER_COPIES) + 44
    tiles = pltpu.VMEM((slots, TILE, TILE), jnp.bfloat16)
    full = (2, 2, 4, 4, 2, KH, TILE)
    scratch = [
        tiles,
        tiles,
        pltpu.VMEM((IT + 1, 2 * KH, TILE), jnp.bfloat16),
        pltpu.VMEM(((slots + UT) // 2, KH, TILE), F32),
        pltpu.VMEM(full, F32),
        pltpu.VMEM((2, UT, KH, TILE), F32),
        pltpu.VMEM((2, UT, KH, TILE), F32),
        pltpu.VMEM(full, F32),
        pltpu.VMEM((16, K, TILE), F32),
        pltpu.VMEM((2, 2, NCH, SIZE, KH, TILE), F32),
        pltpu.VMEM((2, NCH, SIZE, KH, TILE), F32),
        pltpu.VMEM((2, NCH, SIZE, KH, TILE), F32),
        pltpu.VMEM((8, K, K), F32),
        pltpu.VMEM((8, K, K), F32),
        pltpu.VMEM((16, K, K), F32),
        pltpu.VMEM((16, K, K), F32),
        pltpu.VMEM((16, TILE), F32),
        pltpu.SemaphoreType.DMA((LOADS,)),
        *reduce_bufs(),
        *reduce_bufs(),
        pltpu.SemaphoreType.DMA((copies,)),
        pltpu.SemaphoreType.DMA((copies,)),
    ]
    return pl.pallas_call(
        functools.partial(whole_kernel, user_total, item_total),
        out_shape=(
            jax.ShapeDtypeStruct((K, 16 * TILE), F32),
            jax.ShapeDtypeStruct((K, 2 * TILE), F32),
        ),
        in_specs=[SMEM, SMEM, VMEM, VMEM, VMEM, pl.BlockSpec(memory_space=pl.ANY)],
        out_specs=(VMEM, VMEM),
        scratch_shapes=scratch,
        compiler_params=pltpu.CompilerParams(
            collective_id=1, has_side_effects=True, vmem_limit_bytes=VMEM_LIMIT
        ),
        name="cocluster",
    )(order, last, start, user_degree, item_degree, vals)


def slot_order(rows, cols, count):
    slots = rows.shape[0]
    at = jnp.arange(slots, dtype=jnp.int32)
    dead = jnp.where(at < count, 0, UT)
    target = jnp.stack([rows, cols]) + dead
    source = jnp.stack([cols, rows])
    code = (target * IT + source) * slots + at
    rank = jnp.sum((code[:, None, :] < code[:, :, None]).astype(jnp.int32), axis=2)
    line = jnp.arange(UT, dtype=jnp.int32)
    has = jnp.sum((target[:, None, :] == line[None, :, None]).astype(jnp.int32), axis=2)
    odd = has % 2
    moved = jnp.sum(jnp.where(line[None, :, None] < target[:, None, :], odd[:, :, None], 0), axis=1)
    place = jnp.arange(slots + UT, dtype=jnp.int32)[None, :, None]
    ranked = jnp.sum(jnp.where((rank + moved)[:, None, :] == place, code[:, None, :] + 1, 0), axis=2) - 1
    none = ranked < 0
    slot = jnp.where(none, 0, ranked % slots)
    source = jnp.where(none, IT, (ranked // slots) % IT)
    target = ranked // (slots * IT)
    before = jnp.concatenate([jnp.full((2, 2), -1, jnp.int32), target[:, :-2]], axis=1)
    order = jnp.stack([slot, source, (target != before).astype(jnp.int32)], axis=1)
    upto = jnp.sum(jnp.where(line[None, None, :] <= line[None, :, None], (has + odd)[:, None, :], 0), axis=2)
    last = jnp.stack([jnp.maximum(upto // 2 - 1, 0), (has > 0).astype(jnp.int32)], axis=1)
    return order, last


def body(tile_rows, tile_cols, tile_count, tile_vals, user_degree, item_degree, start_items):
    user_total = 16 * TILE * lax.axis_size("users") * lax.axis_size("items")
    item_total = 2 * TILE * lax.axis_size("users") * lax.axis_size("items")
    order, last = slot_order(tile_rows[0, 0], tile_cols[0, 0], tile_count[0, 0])
    degrees = user_degree.reshape(16, TILE), item_degree.reshape(2, TILE)
    return whole_call(user_total, item_total, order, last, start_items, *degrees, tile_vals[0, 0])


def solution(mesh):
    in_specs = (
        P("users", "items", None),
        P("users", "items", None),
        P("users", "items"),
        P("users", "items", None, None, None),
        P(("users", "items")),
        P(("items", "users")),
        P(None, ("items", "users")),
    )
    out_specs = (P(None, ("users", "items")), P(None, ("items", "users")))
    return jax.shard_map(body, mesh=mesh, in_specs=in_specs, out_specs=out_specs, check_vma=False)
```
